512 devices in a mesh: space: 128 (over z_lo, x, y), vec: 4 (over z_hi, core).
Axes of the slice: x: 4, y: 4, z: 16 (z_hi: 2, z_lo: 8; z = z_hi * 8 + z_lo), core: 2. Of those that a mesh axis runs over, the one named last changes fastest.
Arguments:
- vectors: bfloat16 [8, 32, 6, 128, 2048], P(None, 'vec', None, 'space'), may hold values from -3 to 3
- gauge_links: bfloat16 [3, 18, 128, 2048], P(None, None, 'space'), may hold values from -2.5 to 2.5
- momentum: int32 [3], replicated, may hold values from -2 to 2
- directions: int32 [2], replicated, may hold values from 0 to 2, as said below
- blocks: int32 [3], replicated, may hold values from 0 to 7, as said below
Outputs:
- elementals: float32 [2, 32, 1024], P(None, 'vec')
The draws below stay inside these ranges and needn't reach their ends.
Inputs may be any that keep to these rules, and one draw needn't show every extreme that they name: `directions`: at least one of the 2 steps runs along the third dimension, and not all steps share one direction. Three different blocks, among them the first and the last stored block.
All inputs are finite; a program needn't handle non-finite values.
Results may differ from the reference program's by a relative error of at most 0.0075.
Values may be sent and summed in bfloat16 or wider, within the bound.
A program may use at most 64 MiB of HBM per device.

```python
import math
import jax
import jax.numpy as jnp
from jax import lax

NVEC = 32
NBLK = 8
DISP = 2
LX = 32
LY = 64
NZ = 128


def draw_directions(key, part):
    key = jax.random.fold_in(key, 7)
    first_key, second_key = jax.random.split(key)
    picked = jax.random.randint(first_key, (DISP,), 0, 2)
    forced = jax.random.randint(second_key, (), 0, DISP)
    return jnp.where(jnp.arange(DISP) == forced, 2, picked).astype(jnp.int32)


def draw_blocks(key, part):
    key = jax.random.fold_in(key, 11)
    middle_key, order_key = jax.random.split(key)
    middle = jax.random.randint(middle_key, (), 1, NBLK - 1).astype(jnp.int32)
    trio = jnp.stack([jnp.zeros((), jnp.int32), middle, jnp.full((), NBLK - 1, jnp.int32)])
    order = jax.random.permutation(order_key, 3)
    return trio[order].astype(jnp.int32)


def levels(key, dims, cuts, least, largest):
    loudness, own = 1.0, jax.random.fold_in(key, 6)
    for axis_at, blocks in cuts:
        steps = jnp.exp(jax.random.uniform(jax.random.fold_in(own, axis_at), (blocks,), jnp.float32, least / len(cuts), largest / len(cuts)))
        loudness = loudness * jnp.repeat(steps, dims[axis_at] // blocks).reshape([-1 if axis == axis_at else 1 for axis in range(len(dims))])
    return loudness


def scatter_about(key, extent, width, limit, cuts=(), kind=jnp.bfloat16):
    drawn = width * jax.random.normal(key, extent, jnp.float32)
    if cuts:
        drawn = drawn * levels(key, extent, cuts, -0.22, 0.18)
    return jnp.clip(drawn, -limit, limit).astype(kind)


def setup_inputs(seed: int = 0) -> dict:
    keys = jax.random.split(jax.random.key(seed), 6)
    vectors = scatter_about(keys[0], (NBLK, NVEC, 6, NZ, LX * LY), 0.5, 3.0, ((1, 4), (3, 128)))
    gauge_links = scatter_about(keys[1], (3, 18, NZ, LX * LY), 0.41, 2.5, ((2, 128),))
    momentum = jax.random.randint(keys[2], (3,), -2, 3).astype(jnp.int32)
    directions = draw_directions(jax.random.fold_in(keys[5], 71), 0)
    blocks = draw_blocks(jax.random.fold_in(keys[5], 71), 0)
    return {"vectors": vectors, "gauge_links": gauge_links, "momentum": momentum, "directions": directions, "blocks": blocks}


TWO_PI = 2.0 * math.pi

def link_apply(links_now, field):
    comps = []
    for c in range(3):
        real_part = 0.0
        imag_part = 0.0
        for b in range(3):
            link_real = links_now[(c * 3 + b) * 2].astype(jnp.float32)
            link_imag = links_now[(c * 3 + b) * 2 + 1].astype(jnp.float32)
            field_real = field[:, 2 * b].astype(jnp.float32)
            field_imag = field[:, 2 * b + 1].astype(jnp.float32)
            real_part = real_part + link_real * field_real - link_imag * field_imag
            imag_part = imag_part + link_real * field_imag + link_imag * field_real
        comps.append(real_part)
        comps.append(imag_part)
    return jnp.stack(comps, axis=1)

def roll_plane(field, first_axis):
    shape = field.shape
    grid = field.reshape(shape[:-1] + (LX, LY))
    if first_axis:
        moved = jnp.roll(grid, -1, axis=-2)
    else:
        moved = jnp.roll(grid, -1, axis=-1)
    return moved.reshape(shape)

def displace(field, gauge_links, directions):
    for s in range(DISP):
        d = directions[s]
        along_z = jnp.roll(field, -1, axis=-2)
        candidate = jnp.where(d == 0, roll_plane(field, True), jnp.where(d == 1, roll_plane(field, False), along_z))
        field = link_apply(gauge_links[d], candidate).astype(jnp.bfloat16)
    return field

def plane_phases(momentum):
    index = jnp.arange(LX * LY, dtype=jnp.int32)
    x_coord = index // LY
    y_coord = index % LY
    z_coord = jnp.arange(NZ, dtype=jnp.int32)[:, None]
    fraction = (momentum[0] * x_coord % LX).astype(jnp.float32) / LX
    fraction = fraction + (momentum[1] * y_coord % LY).astype(jnp.float32) / LY
    fraction = fraction + (momentum[2] * z_coord % NZ).astype(jnp.float32) / NZ
    angles = TWO_PI * fraction
    return (jnp.cos(angles), jnp.sin(angles))

def apply_phase(field, cosines, sines):
    comps = []
    for a in range(3):
        field_real = field[:, 2 * a].astype(jnp.float32)
        field_imag = field[:, 2 * a + 1].astype(jnp.float32)
        comps.append(cosines * field_real + sines * field_imag)
        comps.append(cosines * field_imag - sines * field_real)
    return jnp.stack(comps, axis=1).astype(jnp.bfloat16)

def cross_table(left, right):
    parts = []
    for a in range(3):
        b = (a + 1) % 3
        c = (a + 2) % 3
        lbr = left[:, 2 * b].astype(jnp.float32)[:, None]
        lbi = left[:, 2 * b + 1].astype(jnp.float32)[:, None]
        lcr = left[:, 2 * c].astype(jnp.float32)[:, None]
        lci = left[:, 2 * c + 1].astype(jnp.float32)[:, None]
        rbr = right[:, 2 * b].astype(jnp.float32)[None]
        rbi = right[:, 2 * b + 1].astype(jnp.float32)[None]
        rcr = right[:, 2 * c].astype(jnp.float32)[None]
        rci = right[:, 2 * c + 1].astype(jnp.float32)[None]
        parts.append((lbr * rcr - lbi * rci - (lcr * rbr - lci * rbi)).astype(jnp.bfloat16))
        parts.append((lbr * rci + lbi * rcr - (lcr * rbi + lci * rbr)).astype(jnp.bfloat16))
    table = jnp.concatenate(parts, axis=-1)
    return table.reshape(left.shape[0] * right.shape[0], -1)

def contract(qfield, left, right):
    table = cross_table(left, right).astype(jnp.float32)
    real_rows = []
    imag_rows = []
    for a in range(3):
        real_rows += [qfield[:, 2 * a], -qfield[:, 2 * a + 1]]
        imag_rows += [qfield[:, 2 * a + 1], qfield[:, 2 * a]]
    real_rows = jnp.concatenate(real_rows, axis=-1).astype(jnp.float32)
    imag_rows = jnp.concatenate(imag_rows, axis=-1).astype(jnp.float32)
    real_out = jnp.dot(real_rows, table.T, preferred_element_type=jnp.float32)
    imag_out = jnp.dot(imag_rows, table.T, preferred_element_type=jnp.float32)
    return jnp.stack([real_out, imag_out])

def reference(vectors, gauge_links, momentum, directions, blocks):
    first = vectors[blocks[0]]
    second = vectors[blocks[1]]
    third = vectors[blocks[2]]
    moved = displace(first, gauge_links, directions)
    cosines, sines = plane_phases(momentum)
    phased = apply_phase(moved, cosines, sines)

    def plane_term(pieces):
        return contract(pieces[0], pieces[1], pieces[2])
    terms = lax.map(plane_term, (jnp.moveaxis(phased, 2, 0), jnp.moveaxis(second, 2, 0), jnp.moveaxis(third, 2, 0)))
    total = lax.optimization_barrier(jnp.sum(terms, axis=0))
    return total * (1.0 / math.sqrt(LX * LY * NZ))
```

```python
import functools
import math

import jax
import jax.numpy as jnp
from jax import lax
from jax.experimental import pallas as pl
from jax.experimental.pallas import tpu as pltpu
from jax.sharding import PartitionSpec as P

LX = 32
LY = 64
SITES = LX * LY
PLANES = 128
TWO_PI = 2.0 * math.pi
MESH = pl.DeviceIdType.MESH
F32 = jnp.float32
BF16 = jnp.bfloat16
LANES = 128
QUARTER = SITES // 4
CHUNKS = QUARTER // LANES


def link_rows(links, field):
    out = []
    for c in range(3):
        real_part = None
        for b in range(3):
            at = (c * 3 + b) * 2
            lr = links[at : at + 1]
            li = links[at + 1 : at + 2]
            fr = field[16 * b : 16 * b + 8]
            fi = field[16 * b + 8 : 16 * b + 16]
            re = lr * fr - li * fi
            im = lr * fi + li * fr
            real_part, imag_part = (re, im) if real_part is None else (real_part + re, imag_part + im)
        out += [real_part, imag_part]
    return out


def rolled(direction, row):
    lane = lax.broadcasted_iota(jnp.int32, row.shape, 1)
    next_x = pltpu.roll(row, SITES - LY, 1)
    next_y = jnp.where(
        lax.rem(lane, LY) == LY - 1, pltpu.roll(row, LY - 1, 1), pltpu.roll(row, SITES - 1, 1)
    )
    return jnp.where(direction == 0, next_x, next_y)


def kernel(
    momentum, directions, blocks, vec_hbm, links_hbm, out,
    vec_v, links_v, st_send, st_recv, st_wide, roll_v, shift_send, shift_recv, cos_v, sin_v,
    phi_send, phi_recv, table, e_send, e_recv, z_send, z_recv, ag_recv,
    load_sem, own_sem, shift_sems, st_sems, phi_send_sem, phi_recv_sems, e_sems, z_sems, ag_sems,
):
    space = lax.axis_index("space")
    vec = lax.axis_index("vec")
    flat = lax.rem(space, 16)
    zlow = lax.div(space, 16)
    half = lax.div(vec, 2)
    core = lax.rem(vec, 2)
    zee = half * 8 + zlow

    def flat_peer(d):
        return zlow * 16 + lax.rem(flat + lax.rem(d, 16), 16), half * 2 + lax.rem(core + lax.div(d, 16), 2)

    def z_peer(d):
        z = lax.rem(zee + d, 16)
        return lax.rem(z, 8) * 16 + flat, lax.div(z, 8) * 2 + core

    def vec_peer(d):
        return space, lax.rem(vec + d, 4)

    below = (lax.rem(space + PLANES - 1, PLANES), vec)
    above = (lax.rem(space + 1, PLANES), vec)
    cross_core = (space, (1 - half) * 2 + (1 - core))

    load_vec = pltpu.make_async_copy(vec_hbm, vec_v, load_sem.at[0])
    load_links = pltpu.make_async_copy(links_hbm, links_v, load_sem.at[1])
    load_vec.start()
    load_links.start()

    barrier = pltpu.get_barrier_semaphore()

    def greet(device):
        pl.semaphore_signal(barrier, inc=1, device_id=device, device_id_type=MESH)

    greet(cross_core)

    @pl.loop(1, 16)
    def _(d):
        greet(z_peer(d))

    greet(below)
    greet(above)

    @pl.loop(1, 32)
    def _(d):
        greet(flat_peer(d))

    first_step = directions[0]
    z_first = first_step == 2
    inplane = jnp.where(z_first, directions[1], first_step)

    load_vec.wait()
    load_links.wait()
    for q in range(4):
        at = slice(q * QUARTER, (q + 1) * QUARTER)
        st_send[q, 0:48] = vec_v[blocks[1], :, at]
        st_send[q, 48:96] = vec_v[blocks[2], :, at]

    for b in range(6):
        row = vec_v[blocks[0], (b // 2) * 16 : (b // 2) * 16 + 16, :].astype(F32)
        row = row[(b % 2) * 8 : (b % 2) * 8 + 8]
        roll_v[b * 8 : b * 8 + 8] = rolled(inplane, row)

    @pl.loop(0, SITES // 256)
    def _(t):
        at = pl.ds(t * 256, 256)
        links = links_v[inplane, :, at].astype(F32)
        moved = jnp.concatenate(link_rows(links, roll_v[:, at]), axis=0).astype(BF16)
        shift_send[:, at] = jnp.where(z_first, vec_v[blocks[0], :, at], moved)

    site = lax.broadcasted_iota(jnp.int32, (8, SITES), 1)
    fraction = ((momentum[0] * lax.div(site, LY)) & (LX - 1)).astype(F32) / LX
    fraction = fraction + ((momentum[1] * lax.rem(site, LY)) & (LY - 1)).astype(F32) / LY
    fraction = fraction + ((momentum[2] * space) & (PLANES - 1)).astype(F32) / PLANES
    angles = TWO_PI * fraction
    cos_v[...] = jnp.cos(angles)
    sin_v[...] = jnp.sin(angles)

    pl.semaphore_wait(barrier, 15 + 31 + 3)

    shift = pltpu.make_async_remote_copy(
        src_ref=shift_send, dst_ref=shift_recv, send_sem=shift_sems.at[0], recv_sem=shift_sems.at[1],
        device_id=below, device_id_type=MESH,
    )
    shift.start()
    for d in (2, 1, 3):
        target = lax.rem(vec + d, 4)
        pltpu.make_async_remote_copy(
            src_ref=st_send.at[target], dst_ref=st_recv.at[vec], send_sem=st_sems.at[0],
            recv_sem=st_sems.at[1], device_id=vec_peer(d), device_id_type=MESH,
        ).start()
    own_st = pltpu.make_async_copy(st_send.at[vec], st_recv.at[vec], own_sem.at[0])
    own_st.start()

    shift.wait_recv()

    @pl.loop(0, SITES // 256)
    def _(t):
        at = pl.ds(t * 256, 256)
        links = links_v[2, :, at].astype(F32)
        moved = jnp.concatenate(link_rows(links, shift_recv[:, at].astype(F32)), axis=0)
        shift_recv[:, at] = moved.astype(BF16)

    for b in range(6):
        row = shift_recv[(b // 2) * 16 : (b // 2) * 16 + 16, :].astype(F32)
        row = row[(b % 2) * 8 : (b % 2) * 8 + 8]
        roll_v[b * 8 : b * 8 + 8] = rolled(inplane, row)

    @pl.loop(0, SITES // LANES)
    def _(t):
        at = pl.ds(t * LANES, LANES)
        links = links_v[inplane, :, at].astype(F32)
        moved = jnp.concatenate(link_rows(links, roll_v[:, at]), axis=0).astype(BF16)
        moved = jnp.where(z_first, moved, shift_recv[:, at]).astype(F32)
        cosines = cos_v[:, at]
        sines = sin_v[:, at]
        rows = []
        for a in range(3):
            re = moved[16 * a : 16 * a + 8]
            im = moved[16 * a + 8 : 16 * a + 16]
            rows += [cosines * re + sines * im, cosines * im - sines * re]
        phi_send[lax.rem(t, CHUNKS), lax.div(t, CHUNKS)] = jnp.concatenate(rows, axis=0).astype(BF16)

    st_three = st_recv.at[pl.ds(0, 3)]
    pltpu.make_async_copy(st_three, st_three, st_sems.at[0]).wait()
    for n in range(CHUNKS):
        for d in (2, 1, 3):
            target = lax.rem(vec + d, 4)
            pltpu.make_async_remote_copy(
                src_ref=phi_send.at[n, target], dst_ref=phi_recv.at[n, vec], send_sem=phi_send_sem.at[0],
                recv_sem=phi_recv_sems.at[n], device_id=vec_peer(d), device_id_type=MESH,
            ).start()
    own_phi = []
    for n in range(CHUNKS):
        own_phi.append(pltpu.make_async_copy(phi_send.at[n, vec], phi_recv.at[n, vec], own_sem.at[1 + n]))
        own_phi[-1].start()

    own_st.wait()
    pltpu.make_async_copy(st_three, st_three, st_sems.at[1]).wait()

    @pl.loop(0, 4)
    def _(source):
        st_wide[source] = st_recv[source].astype(F32)

    @pl.loop(0, CHUNKS * 4)
    def _(turn):
        n = lax.div(turn, 4)
        source = lax.rem(turn, 4)
        at = pl.ds(n * LANES, LANES)
        right = [[st_wide[k, 48 + 8 * b : 56 + 8 * b, at] for b in range(6)] for k in range(4)]
        for j in range(8):
            left = [
                jnp.broadcast_to(st_wide[source, 8 * b + j : 8 * b + j + 1, at], (8, LANES)) for b in range(6)
            ]
            start = source * 256 + j * 32
            for a in range(3):
                b = 2 * ((a + 1) % 3)
                c = 2 * ((a + 2) % 3)
                reals = []
                imags = []
                for k in range(4):
                    rbr, rbi, rcr, rci = right[k][b], right[k][b + 1], right[k][c], right[k][c + 1]
                    lbr, lbi, lcr, lci = left[b], left[b + 1], left[c], left[c + 1]
                    reals.append(lbr * rcr - lbi * rci - (lcr * rbr - lci * rbi))
                    imags.append(lbr * rci + lbi * rcr - (lcr * rbi + lci * rbr))
                table[n, pl.ds(start, 32), 2 * a * LANES : (2 * a + 1) * LANES] = jnp.concatenate(
                    reals, axis=0
                ).astype(BF16)
                table[n, pl.ds(start, 32), (2 * a + 1) * LANES : (2 * a + 2) * LANES] = jnp.concatenate(
                    imags, axis=0
                ).astype(BF16)

    total = None
    for n in range(CHUNKS):
        own_phi[n].wait()
        phi_three = phi_recv.at[n, pl.ds(0, 3)]
        pltpu.make_async_copy(phi_three, phi_three, phi_recv_sems.at[n]).wait()
        real_rows = []
        imag_rows = []
        for source in range(4):
            field = phi_recv[n, source].astype(F32)
            reals = [field[16 * a : 16 * a + 8] for a in range(3)]
            imags = [field[16 * a + 8 : 16 * a + 16] for a in range(3)]
            real_rows.append(jnp.concatenate([x for a in range(3) for x in (reals[a], -imags[a])], axis=1))
            imag_rows.append(jnp.concatenate([x for a in range(3) for x in (imags[a], reals[a])], axis=1))
        rows = jnp.concatenate(real_rows + imag_rows, axis=0).astype(BF16)
        term = lax.dot_general(rows, table[n], (((1,), (1,)), ((), ())), preferred_element_type=F32)
        total = term if total is None else total + term
    for part in range(2):
        for h in range(2):
            for c in range(2):
                at = part * 32 + (2 * h + c) * 8
                for tile in range(8):
                    e_send[c, part * 8 + tile, h] = total[at : at + 8, tile * LANES : (tile + 1) * LANES]

    @pl.loop(1, 32)
    def _(d):
        to_space, to_vec = flat_peer(d)
        pltpu.make_async_remote_copy(
            src_ref=e_send.at[lax.rem(to_vec, 2), lax.rem(to_space, 16)], dst_ref=e_recv.at[d - 1],
            send_sem=e_sems.at[0], recv_sem=e_sems.at[1], device_id=(to_space, to_vec), device_id_type=MESH,
        ).start()

    plane_sum = e_send[core, flat]
    pltpu.make_async_copy(e_recv, e_recv, e_sems.at[1]).wait()
    for d in range(31):
        plane_sum = plane_sum + e_recv[d]
    z_send[...] = plane_sum

    @pl.loop(1, 16)
    def _(d):
        to_space, to_vec = z_peer(d)
        pltpu.make_async_remote_copy(
            src_ref=z_send.at[lax.div(to_vec, 2)], dst_ref=z_recv.at[zee], send_sem=z_sems.at[0],
            recv_sem=z_sems.at[1], device_id=(to_space, to_vec), device_id_type=MESH,
        ).start()

    z_recv[zee] = z_send[half]
    z_others = z_recv.at[pl.ds(0, 15)]
    pltpu.make_async_copy(z_others, z_others, z_sems.at[1]).wait()
    whole = z_recv[0]
    for z in range(1, 16):
        whole = whole + z_recv[z]
    ag_recv[flat] = whole * (1.0 / math.sqrt(SITES * PLANES))

    @pl.loop(1, 16)
    def _(d):
        pltpu.make_async_remote_copy(
            src_ref=ag_recv.at[flat], dst_ref=ag_recv.at[flat], send_sem=ag_sems.at[0],
            recv_sem=ag_sems.at[1], device_id=flat_peer(d), device_id_type=MESH,
        ).start()

    ag_others = ag_recv.at[pl.ds(0, 15)]
    pltpu.make_async_copy(ag_others, ag_others, ag_sems.at[1]).wait()
    for part in range(2):
        for tile in range(8):
            out[part, :, tile * LANES : (tile + 1) * LANES] = ag_recv[part * 8 + tile]

    shift.wait_send()
    phi_three = phi_recv.at[:, pl.ds(0, 3)]
    pltpu.make_async_copy(phi_three, phi_three, phi_send_sem.at[0]).wait()
    pltpu.make_async_copy(e_recv, e_recv, e_sems.at[0]).wait()
    pltpu.make_async_copy(z_others, z_others, z_sems.at[0]).wait()
    pltpu.make_async_copy(ag_others, ag_others, ag_sems.at[0]).wait()


def shards(vectors, gauge_links, momentum, directions, blocks):
    nblk = vectors.shape[0]
    vec = vectors.transpose(0, 2, 3, 1, 4).reshape(nblk, 48, SITES)
    links = gauge_links.reshape(3, 18, SITES)
    smem = pl.BlockSpec(memory_space=pltpu.SMEM)
    return pl.pallas_call(
        kernel,
        name="elementals",
        out_shape=jax.ShapeDtypeStruct((2, 8, 1024), F32),
        in_specs=[smem, smem, smem, pl.BlockSpec(memory_space=pl.ANY), pl.BlockSpec(memory_space=pl.ANY)],
        out_specs=pl.BlockSpec(memory_space=pltpu.VMEM),
        scratch_shapes=[
            pltpu.VMEM((nblk, 48, SITES), BF16),
            pltpu.VMEM((3, 18, SITES), BF16),
            pltpu.VMEM((4, 96, QUARTER), BF16),
            pltpu.VMEM((4, 96, QUARTER), BF16),
            pltpu.VMEM((4, 96, QUARTER), F32),
            pltpu.VMEM((48, SITES), F32),
            pltpu.VMEM((48, SITES), BF16),
            pltpu.VMEM((48, SITES), BF16),
            pltpu.VMEM((8, SITES), F32),
            pltpu.VMEM((8, SITES), F32),
            pltpu.VMEM((CHUNKS, 4, 48, LANES), BF16),
            pltpu.VMEM((CHUNKS, 4, 48, LANES), BF16),
            pltpu.VMEM((CHUNKS, 1024, 6 * LANES), BF16),
            pltpu.VMEM((2, 16, 2, 8, LANES), F32),
            pltpu.VMEM((31, 2, 8, LANES), F32),
            pltpu.VMEM((2, 8, LANES), F32),
            pltpu.VMEM((16, 8, LANES), F32),
            pltpu.VMEM((16, 8, LANES), F32),
            pltpu.SemaphoreType.DMA((2,)),
            pltpu.SemaphoreType.DMA((1 + CHUNKS,)),
            pltpu.SemaphoreType.DMA((2,)),
            pltpu.SemaphoreType.DMA((2,)),
            pltpu.SemaphoreType.DMA((1,)),
            pltpu.SemaphoreType.DMA((CHUNKS,)),
            pltpu.SemaphoreType.DMA((2,)),
            pltpu.SemaphoreType.DMA((2,)),
            pltpu.SemaphoreType.DMA((2,)),
        ],
        compiler_params=pltpu.CompilerParams(
            collective_id=1, has_side_effects=True, vmem_limit_bytes=40 * 2**20
        ),
    )(momentum, directions, blocks, vec, links)


def solution(mesh):
    in_specs = (P(None, "vec", None, "space", None), P(None, None, "space", None), P(), P(), P())
    out_specs = P(None, "vec", None)
    return jax.shard_map(shards, mesh=mesh, in_specs=in_specs, out_specs=out_specs, check_vma=False)
```

```python
import functools
import math

import jax
import jax.numpy as jnp
from jax import lax
from jax.experimental import pallas as pl
from jax.experimental.pallas import tpu as pltpu
from jax.sharding import PartitionSpec as P

LX = 32
LY = 64
SITES = LX * LY
PLANES = 128
TWO_PI = 2.0 * math.pi
MESH = pl.DeviceIdType.MESH
F32 = jnp.float32
BF16 = jnp.bfloat16
LANES = 128
QUARTER = SITES // 4
CHUNKS = QUARTER // LANES
FLAT_ORDER = sorted(range(1, 32), key=lambda d: -(min(d // 4 % 4, 4 - d // 4 % 4) + min(d % 4, 4 - d % 4)))


def link_rows(links, field):
    out = []
    for c in range(3):
        real_part = None
        for b in range(3):
            at = (c * 3 + b) * 2
            lr = links[at : at + 1]
            li = links[at + 1 : at + 2]
            fr = field[16 * b : 16 * b + 8]
            fi = field[16 * b + 8 : 16 * b + 16]
            re = lr * fr - li * fi
            im = lr * fi + li * fr
            real_part, imag_part = (re, im) if real_part is None else (real_part + re, imag_part + im)
        out += [real_part, imag_part]
    return out


def rolled(direction, row):
    lane = lax.broadcasted_iota(jnp.int32, row.shape, 1)
    next_x = pltpu.roll(row, SITES - LY, 1)
    next_y = jnp.where(
        lax.rem(lane, LY) == LY - 1, pltpu.roll(row, LY - 1, 1), pltpu.roll(row, SITES - 1, 1)
    )
    return jnp.where(direction == 0, next_x, next_y)


def kernel(
    momentum_hbm, directions_hbm, blocks_hbm, vec_hbm, links_hbm, out,
    momentum, directions, blocks, vec_v, links_v, st_send, st_recv, st_wide, roll_v, shift_send, shift_recv, cos_v, sin_v,
    phi_send, phi_recv, table, e_send, e_recv, z_send, z_recv, ag_recv,
    load_sem, own_sem, shift_sems, st_sems, phi_send_sem, phi_recv_sems, e_sems, z_sems, ag_sems, known_sems,
):
    space = lax.axis_index("space")
    vec = lax.axis_index("vec")
    flat = lax.rem(space, 16)
    zlow = lax.div(space, 16)
    half = lax.div(vec, 2)
    core = lax.rem(vec, 2)
    zee = half * 8 + zlow

    def flat_peer(d):
        x = lax.rem(lax.div(flat, 4) + lax.rem(lax.div(d, 4), 4), 4)
        y = lax.rem(flat + lax.rem(d, 4), 4)
        return zlow * 16 + x * 4 + y, half * 2 + lax.rem(core + lax.div(d, 16), 2)

    def z_peer(d):
        z = lax.rem(zee + d, 16)
        return lax.rem(z, 8) * 16 + flat, lax.div(z, 8) * 2 + core

    def vec_peer(d):
        return space, lax.rem(vec + d, 4)

    below = (lax.rem(space + PLANES - 1, PLANES), vec)
    above = (lax.rem(space + 1, PLANES), vec)
    near = half * 2 + (1 - core)
    cross_core = (space, (1 - half) * 2 + (1 - core))

    barrier = pltpu.get_barrier_semaphore()

    def greet(device):
        pl.semaphore_signal(barrier, inc=1, device_id=device, device_id_type=MESH)

    greet(z_peer(8))
    greet(cross_core)
    greet(z_peer(1))
    greet(z_peer(15))
    greet(below)
    greet(above)

    @pl.loop(1, 32)
    def _(d):
        greet(flat_peer(d))

    loads = [
        pltpu.make_async_copy(source, target, load_sem.at[at])
        for at, (source, target) in enumerate(
            (
                (blocks_hbm, blocks), (vec_hbm, vec_v), (links_hbm, links_v),
                (directions_hbm, directions), (momentum_hbm, momentum),
            )
        )
    ]
    for load in loads:
        load.start()
    for load in loads:
        load.wait()

    def pass_on(at, steps):
        for d in (steps, 16 - steps):
            pl.semaphore_signal(known_sems.at[at], inc=1, device_id=z_peer(d), device_id_type=MESH)

    first_step = directions[0]
    z_first = first_step == 2
    inplane = jnp.where(z_first, directions[1], first_step)

    for q in range(4):
        at = slice(q * QUARTER, (q + 1) * QUARTER)
        st_send[q, 0:48] = vec_v[blocks[1], :, at]
        st_send[q, 48:96] = vec_v[blocks[2], :, at]

    pl.semaphore_wait(barrier, 31 + 6)

    for d in (2, 1, 3):
        target = lax.rem(vec + d, 4)
        pltpu.make_async_remote_copy(
            src_ref=st_send.at[target], dst_ref=st_recv.at[vec], send_sem=st_sems.at[0],
            recv_sem=st_sems.at[1], device_id=vec_peer(d), device_id_type=MESH,
        ).start()
    pass_on(0, 1)
    own_st = pltpu.make_async_copy(st_send.at[vec], st_recv.at[vec], own_sem.at[0])
    own_st.start()

    for b in range(6):
        row = vec_v[blocks[0], (b // 2) * 16 : (b // 2) * 16 + 16, :].astype(F32)
        row = row[(b % 2) * 8 : (b % 2) * 8 + 8]
        roll_v[b * 8 : b * 8 + 8] = rolled(inplane, row)

    @pl.loop(0, SITES // 256)
    def _(t):
        at = pl.ds(t * 256, 256)
        links = links_v[inplane, :, at].astype(F32)
        moved = jnp.concatenate(link_rows(links, roll_v[:, at]), axis=0).astype(BF16)
        shift_send[:, at] = jnp.where(z_first, vec_v[blocks[0], :, at], moved)

    shift = pltpu.make_async_remote_copy(
        src_ref=shift_send, dst_ref=shift_recv, send_sem=shift_sems.at[0], recv_sem=shift_sems.at[1],
        device_id=below, device_id_type=MESH,
    )
    shift.start()
    pl.semaphore_wait(known_sems.at[0], 2)
    pass_on(1, 2)
    site = lax.broadcasted_iota(jnp.int32, (8, SITES), 1)
    fraction = ((momentum[0] * lax.div(site, LY)) & (LX - 1)).astype(F32) / LX
    fraction = fraction + ((momentum[1] * lax.rem(site, LY)) & (LY - 1)).astype(F32) / LY
    fraction = fraction + ((momentum[2] * space) & (PLANES - 1)).astype(F32) / PLANES
    angles = TWO_PI * fraction
    cos_v[...] = jnp.cos(angles)
    sin_v[...] = jnp.sin(angles)

    shift.wait_recv()
    pl.semaphore_wait(known_sems.at[1], 2)
    pass_on(2, 4)

    @pl.loop(0, SITES // 256)
    def _(t):
        at = pl.ds(t * 256, 256)
        links = links_v[2, :, at].astype(F32)
        moved = jnp.concatenate(link_rows(links, shift_recv[:, at].astype(F32)), axis=0)
        shift_recv[:, at] = moved.astype(BF16)

    for b in range(6):
        row = shift_recv[(b // 2) * 16 : (b // 2) * 16 + 16, :].astype(F32)
        row = row[(b % 2) * 8 : (b % 2) * 8 + 8]
        roll_v[b * 8 : b * 8 + 8] = rolled(inplane, row)

    @pl.loop(0, SITES // LANES)
    def _(t):
        at = pl.ds(t * LANES, LANES)
        links = links_v[inplane, :, at].astype(F32)
        moved = jnp.concatenate(link_rows(links, roll_v[:, at]), axis=0).astype(BF16)
        moved = jnp.where(z_first, moved, shift_recv[:, at]).astype(F32)
        cosines = cos_v[:, at]
        sines = sin_v[:, at]
        rows = []
        for a in range(3):
            re = moved[16 * a : 16 * a + 8]
            im = moved[16 * a + 8 : 16 * a + 16]
            rows += [cosines * re + sines * im, cosines * im - sines * re]
        phi_send[lax.rem(t, CHUNKS), lax.div(t, CHUNKS)] = jnp.concatenate(rows, axis=0).astype(BF16)

    for n in range(CHUNKS):
        for d, sem in ((2, phi_recv_sems.at[n]), (None, phi_recv_sems.at[n]), (1, phi_recv_sems.at[CHUNKS])):
            to_vec = near if d == 1 else (lax.rem(vec + 2, 4) if d == 2 else cross_core[1])
            pltpu.make_async_remote_copy(
                src_ref=phi_send.at[n, to_vec], dst_ref=phi_recv.at[n, vec], send_sem=phi_send_sem.at[0],
                recv_sem=sem, device_id=(space, to_vec), device_id_type=MESH,
            ).start()
    own_phi = pltpu.make_async_copy(phi_send.at[:, vec], phi_recv.at[:, vec], own_sem.at[1])
    own_phi.start()

    pl.semaphore_wait(known_sems.at[2], 2)
    st_three = st_recv.at[pl.ds(0, 3)]
    own_st.wait()
    pltpu.make_async_copy(st_three, st_three, st_sems.at[1]).wait()

    @pl.loop(0, 4)
    def _(source):
        st_wide[source] = st_recv[source].astype(F32)

    @pl.loop(0, CHUNKS * 4)
    def _(turn):
        n = lax.div(turn, 4)
        source = lax.rem(turn, 4)
        at = pl.ds(n * LANES, LANES)
        right = [[st_wide[k, 48 + 8 * b : 56 + 8 * b, at] for b in range(6)] for k in range(4)]
        for j in range(8):
            left = [
                jnp.broadcast_to(st_wide[source, 8 * b + j : 8 * b + j + 1, at], (8, LANES)) for b in range(6)
            ]
            start = source * 256 + j * 32
            for a in range(3):
                b = 2 * ((a + 1) % 3)
                c = 2 * ((a + 2) % 3)
                reals = []
                imags = []
                for k in range(4):
                    rbr, rbi, rcr, rci = right[k][b], right[k][b + 1], right[k][c], right[k][c + 1]
                    lbr, lbi, lcr, lci = left[b], left[b + 1], left[c], left[c + 1]
                    reals.append(lbr * rcr - lbi * rci - (lcr * rbr - lci * rbi))
                    imags.append(lbr * rci + lbi * rcr - (lcr * rbi + lci * rbr))
                table[n, pl.ds(start, 32), 2 * a * LANES : (2 * a + 1) * LANES] = jnp.concatenate(
                    reals, axis=0
                ).astype(BF16)
                table[n, pl.ds(start, 32), (2 * a + 1) * LANES : (2 * a + 2) * LANES] = jnp.concatenate(
                    imags, axis=0
                ).astype(BF16)

    def product(n, whose):
        real_rows = []
        imag_rows = []
        for c in range(2):
            field = phi_recv[n, 2 * whose + c].astype(F32)
            reals = [field[16 * a : 16 * a + 8] for a in range(3)]
            imags = [field[16 * a + 8 : 16 * a + 16] for a in range(3)]
            real_rows.append(jnp.concatenate([x for a in range(3) for x in (reals[a], -imags[a])], axis=1))
            imag_rows.append(jnp.concatenate([x for a in range(3) for x in (imags[a], reals[a])], axis=1))
        rows = jnp.concatenate(real_rows + imag_rows, axis=0).astype(BF16)
        return lax.dot_general(rows, table[n], (((1,), (1,)), ((), ())), preferred_element_type=F32)

    def scatter(at, total):
        for part in range(2):
            for c in range(2):
                start = part * 16 + c * 8
                for tile in range(8):
                    e_send[at, c, part * 8 + tile] = total[start : start + 8, tile * LANES : (tile + 1) * LANES]
        for d in FLAT_ORDER:
            to_space, to_vec = flat_peer(d)
            pltpu.make_async_remote_copy(
                src_ref=e_send.at[at, lax.rem(to_vec, 2), lax.rem(to_space, 16)], dst_ref=e_recv.at[at, d - 1],
                send_sem=e_sems.at[2], recv_sem=e_sems.at[at], device_id=(to_space, to_vec), device_id_type=MESH,
            ).start()

    def gathered(at):
        pltpu.make_async_copy(e_recv.at[at], e_recv.at[at], e_sems.at[at]).wait()
        total = e_send[at, core, flat]
        for d in range(31):
            total = total + e_recv[at, d]
        return total

    def send_z(at, d):
        to_space, to_vec = z_peer(d)
        pltpu.make_async_remote_copy(
            src_ref=z_send.at[at], dst_ref=z_recv.at[zee], send_sem=z_sems.at[2],
            recv_sem=z_sems.at[at], device_id=(to_space, to_vec), device_id_type=MESH,
        ).start()

    own_phi.wait()
    phi_near = phi_recv.at[:, 0]
    pltpu.make_async_copy(phi_near, phi_near, phi_recv_sems.at[CHUNKS]).wait()
    total = product(0, half)
    for n in range(1, CHUNKS):
        total = total + product(n, half)
    scatter(0, total)

    total = None
    for n in range(CHUNKS):
        phi_two = phi_recv.at[n, pl.ds(0, 2)]
        pltpu.make_async_copy(phi_two, phi_two, phi_recv_sems.at[n]).wait()
        term = product(n, 1 - half)
        total = term if total is None else total + term
    scatter(1, total)

    z_send[0] = gathered(0)
    z_recv[zee] = z_send[0]
    for step in range(1, 8):
        send_z(0, half * 8 + lax.rem(zlow + step, 8) - zee + 16)

    z_send[1] = gathered(1)
    for step in (0, 1, 7, 2, 6, 3, 5, 4):
        send_z(1, (1 - half) * 8 + lax.rem(zlow + step, 8) - zee + 16)

    z_same = z_recv.at[pl.ds(0, 7)]
    z_other = z_recv.at[pl.ds(0, 8)]
    pltpu.make_async_copy(z_same, z_same, z_sems.at[0]).wait()
    pltpu.make_async_copy(z_other, z_other, z_sems.at[1]).wait()
    whole = z_recv[0]
    for z in range(1, 16):
        whole = whole + z_recv[z]
    ag_recv[flat] = whole * (1.0 / math.sqrt(SITES * PLANES))

    for d in FLAT_ORDER:
        if d < 16:
            pltpu.make_async_remote_copy(
                src_ref=ag_recv.at[flat], dst_ref=ag_recv.at[flat], send_sem=ag_sems.at[0],
                recv_sem=ag_sems.at[1], device_id=flat_peer(d), device_id_type=MESH,
            ).start()

    ag_others = ag_recv.at[pl.ds(0, 15)]
    pltpu.make_async_copy(ag_others, ag_others, ag_sems.at[1]).wait()
    for part in range(2):
        for tile in range(8):
            out[part, :, tile * LANES : (tile + 1) * LANES] = ag_recv[part * 8 + tile]

    pltpu.make_async_copy(st_three, st_three, st_sems.at[0]).wait()
    shift.wait_send()
    phi_three = phi_recv.at[:, pl.ds(0, 3)]
    pltpu.make_async_copy(phi_three, phi_three, phi_send_sem.at[0]).wait()
    pltpu.make_async_copy(e_recv, e_recv, e_sems.at[2]).wait()
    pltpu.make_async_copy(z_same, z_same, z_sems.at[2]).wait()
    pltpu.make_async_copy(z_other, z_other, z_sems.at[2]).wait()
    pltpu.make_async_copy(ag_others, ag_others, ag_sems.at[0]).wait()


def shards(vectors, gauge_links, momentum, directions, blocks):
    nblk = vectors.shape[0]
    vec = vectors.transpose(0, 2, 3, 1, 4).reshape(nblk, 48, SITES)
    links = gauge_links.reshape(3, 18, SITES)
    return pl.pallas_call(
        kernel,
        name="elementals",
        out_shape=jax.ShapeDtypeStruct((2, 8, 1024), F32),
        in_specs=[pl.BlockSpec(memory_space=pl.ANY)] * 5,
        out_specs=pl.BlockSpec(memory_space=pltpu.VMEM),
        scratch_shapes=[
            pltpu.SMEM((3,), jnp.int32),
            pltpu.SMEM((2,), jnp.int32),
            pltpu.SMEM((3,), jnp.int32),
            pltpu.VMEM((nblk, 48, SITES), BF16),
            pltpu.VMEM((3, 18, SITES), BF16),
            pltpu.VMEM((4, 96, QUARTER), BF16),
            pltpu.VMEM((4, 96, QUARTER), BF16),
            pltpu.VMEM((4, 96, QUARTER), F32),
            pltpu.VMEM((48, SITES), F32),
            pltpu.VMEM((48, SITES), BF16),
            pltpu.VMEM((48, SITES), BF16),
            pltpu.VMEM((8, SITES), F32),
            pltpu.VMEM((8, SITES), F32),
            pltpu.VMEM((CHUNKS, 4, 48, LANES), BF16),
            pltpu.VMEM((CHUNKS, 4, 48, LANES), BF16),
            pltpu.VMEM((CHUNKS, 1024, 6 * LANES), BF16),
            pltpu.VMEM((2, 2, 16, 8, LANES), F32),
            pltpu.VMEM((2, 31, 8, LANES), F32),
            pltpu.VMEM((2, 8, LANES), F32),
            pltpu.VMEM((16, 8, LANES), F32),
            pltpu.VMEM((16, 8, LANES), F32),
            pltpu.SemaphoreType.DMA((5,)),
            pltpu.SemaphoreType.DMA((2,)),
            pltpu.SemaphoreType.DMA((2,)),
            pltpu.SemaphoreType.DMA((2,)),
            pltpu.SemaphoreType.DMA((1,)),
            pltpu.SemaphoreType.DMA((CHUNKS + 1,)),
            pltpu.SemaphoreType.DMA((3,)),
            pltpu.SemaphoreType.DMA((3,)),
            pltpu.SemaphoreType.DMA((2,)),
            pltpu.SemaphoreType.REGULAR((3,)),
        ],
        compiler_params=pltpu.CompilerParams(
            collective_id=1, has_side_effects=True, vmem_limit_bytes=63 * 2**20
        ),
    )(momentum, directions, blocks, vec, links)


def solution(mesh):
    in_specs = (P(None, "vec", None, "space", None), P(None, None, "space", None), P(), P(), P())
    out_specs = P(None, "vec", None)
    return jax.shard_map(shards, mesh=mesh, in_specs=in_specs, out_specs=out_specs, check_vma=False)
```

```python
import functools
import math

import jax
import jax.numpy as jnp
from jax import lax
from jax.experimental import pallas as pl
from jax.experimental.pallas import tpu as pltpu
from jax.sharding import PartitionSpec as P

LX = 32
LY = 64
SITES = LX * LY
PLANES = 128
TWO_PI = 2.0 * math.pi
MESH = pl.DeviceIdType.MESH
F32 = jnp.float32
BF16 = jnp.bfloat16
LANES = 128
QUARTER = SITES // 4
CHUNKS = QUARTER // LANES
FLAT_ORDER = sorted(range(1, 32), key=lambda d: -(min(d // 4 % 4, 4 - d // 4 % 4) + min(d % 4, 4 - d % 4)))


def link_rows(links, field):
    out = []
    for c in range(3):
        real_part = None
        for b in range(3):
            at = (c * 3 + b) * 2
            lr = links[at : at + 1]
            li = links[at + 1 : at + 2]
            fr = field[16 * b : 16 * b + 8]
            fi = field[16 * b + 8 : 16 * b + 16]
            re = lr * fr - li * fi
            im = lr * fi + li * fr
            real_part, imag_part = (re, im) if real_part is None else (real_part + re, imag_part + im)
        out += [real_part, imag_part]
    return out


def rolled(direction, row):
    lane = lax.broadcasted_iota(jnp.int32, row.shape, 1)
    next_x = pltpu.roll(row, SITES - LY, 1)
    next_y = jnp.where(
        lax.rem(lane, LY) == LY - 1, pltpu.roll(row, LY - 1, 1), pltpu.roll(row, SITES - 1, 1)
    )
    return jnp.where(direction == 0, next_x, next_y)


def kernel(
    momentum_hbm, directions_hbm, blocks_hbm, vec_hbm, links_hbm, out,
    momentum, directions, blocks, vec_v, links_v, st_send, st_recv, st_wide, roll_v, shift_send, shift_recv, piece, piece_low, cos_v, sin_v,
    phi_send, phi_recv, table, e_send, e_recv, z_send, z_recv, ag_recv,
    load_sem, own_sem, shift_sems, st_sems, phi_send_sem, phi_recv_sems, e_sems, z_sems, ag_sems, known_sems,
):
    space = lax.axis_index("space")
    vec = lax.axis_index("vec")
    flat = lax.rem(space, 16)
    zlow = lax.div(space, 16)
    half = lax.div(vec, 2)
    core = lax.rem(vec, 2)
    zee = half * 8 + zlow

    def flat_peer(d):
        x = lax.rem(lax.div(flat, 4) + lax.rem(lax.div(d, 4), 4), 4)
        y = lax.rem(flat + lax.rem(d, 4), 4)
        return zlow * 16 + x * 4 + y, half * 2 + lax.rem(core + lax.div(d, 16), 2)

    def z_peer(d):
        z = lax.rem(zee + d, 16)
        return lax.rem(z, 8) * 16 + flat, lax.div(z, 8) * 2 + core

    def vec_peer(d):
        return space, lax.rem(vec + d, 4)

    layer = zlow * 16
    up = (lax.rem(zlow + 1, 8) * 16 + flat, vec)
    down = (lax.rem(zlow + 7, 8) * 16 + flat, vec)
    last = lax.div(flat, 15)
    near = half * 2 + (1 - core)
    cross_core = (space, (1 - half) * 2 + (1 - core))

    barrier = pltpu.get_barrier_semaphore()

    def greet(device):
        pl.semaphore_signal(barrier, inc=1, device_id=device, device_id_type=MESH)

    greet(z_peer(8))
    greet(cross_core)
    greet(z_peer(1))
    greet(z_peer(15))
    greet(up)

    @pl.loop(1, 32)
    def _(d):
        greet(flat_peer(d))

    loads = [
        pltpu.make_async_copy(source, target, load_sem.at[at])
        for at, (source, target) in enumerate(
            (
                (blocks_hbm, blocks), (vec_hbm, vec_v), (links_hbm, links_v),
                (directions_hbm, directions), (momentum_hbm, momentum),
            )
        )
    ]
    for load in loads:
        load.start()
    for load in loads:
        load.wait()

    def pass_on(at, steps):
        for d in (steps, 16 - steps):
            pl.semaphore_signal(known_sems.at[at], inc=1, device_id=z_peer(d), device_id_type=MESH)

    first_step = directions[0]
    z_first = first_step == 2
    inplane = jnp.where(z_first, directions[1], first_step)

    for q in range(4):
        at = slice(q * QUARTER, (q + 1) * QUARTER)
        st_send[q, 0:48] = vec_v[blocks[1], :, at]
        st_send[q, 48:96] = vec_v[blocks[2], :, at]

    for b in range(6):
        row = vec_v[blocks[0], (b // 2) * 16 : (b // 2) * 16 + 16, :].astype(F32)
        row = row[(b % 2) * 8 : (b % 2) * 8 + 8]
        roll_v[b * 8 : b * 8 + 8] = rolled(inplane, row)

    @pl.loop(0, SITES // 256)
    def _(t):
        at = pl.ds(t * 256, 256)
        links = links_v[inplane, :, at].astype(F32)
        moved = jnp.concatenate(link_rows(links, roll_v[:, at]), axis=0).astype(BF16)
        shift_send[:, at] = jnp.where(z_first, vec_v[blocks[0], :, at], moved)

    pl.semaphore_wait(barrier, 31 + 5)

    @pl.when(flat != 0)
    def _():
        pltpu.make_async_remote_copy(
            src_ref=shift_send, dst_ref=shift_recv, send_sem=shift_sems.at[0], recv_sem=shift_sems.at[1],
            device_id=(space - 1, vec), device_id_type=MESH,
        ).start()

    @pl.when(flat == 0)
    def _():
        pltpu.make_async_copy(shift_send.at[:, pl.ds(0, LANES)], piece, shift_sems.at[2]).start()
        for k in range(15, 0, -1):
            pltpu.make_async_remote_copy(
                src_ref=shift_send.at[:, pl.ds(k * LANES, LANES)], dst_ref=piece, send_sem=shift_sems.at[0],
                recv_sem=shift_sems.at[2], device_id=(layer + k, vec), device_id_type=MESH,
            ).start()

    def exchange(role):
        rows = pl.ds(role * 48, 48)
        for d in (2, 1, 3):
            target = lax.rem(vec + d, 4)
            pltpu.make_async_remote_copy(
                src_ref=st_send.at[target, rows], dst_ref=st_recv.at[vec, rows], send_sem=st_sems.at[0],
                recv_sem=st_sems.at[1], device_id=vec_peer(d), device_id_type=MESH,
            ).start()

    exchange(0)
    pass_on(0, 1)
    own_st = pltpu.make_async_copy(st_send.at[vec], st_recv.at[vec], own_sem.at[0])
    own_st.start()

    pl.semaphore_wait(known_sems.at[0], 2)
    pass_on(1, 2)
    site = lax.broadcasted_iota(jnp.int32, (8, SITES), 1)
    fraction = ((momentum[0] * lax.div(site, LY)) & (LX - 1)).astype(F32) / LX
    fraction = fraction + ((momentum[1] * lax.rem(site, LY)) & (LY - 1)).astype(F32) / LY
    fraction = fraction + ((momentum[2] * space) & (PLANES - 1)).astype(F32) / PLANES
    angles = TWO_PI * fraction
    cos_v[...] = jnp.cos(angles)
    sin_v[...] = jnp.sin(angles)

    pltpu.make_async_copy(piece, piece, shift_sems.at[2]).wait()

    def forward(dst, sem):
        pltpu.make_async_remote_copy(
            src_ref=piece, dst_ref=dst, send_sem=shift_sems.at[3], recv_sem=sem, device_id=down, device_id_type=MESH,
        ).start()

    @pl.when(flat != 15)
    def _():
        forward(piece_low, shift_sems.at[4])

    @pl.when(flat == 15)
    def _():
        forward(shift_recv.at[:, pl.ds(15 * LANES, LANES)], shift_sems.at[1])

    exchange(1)
    pl.semaphore_wait(known_sems.at[1], 2)
    pass_on(2, 4)

    def phase_own():
        pltpu.make_async_copy(shift_recv, shift_recv, shift_sems.at[1]).wait()

        @pl.loop(0, SITES // 256)
        def _(t):
            at = pl.ds(t * 256, 256)
            links = links_v[2, :, at].astype(F32)
            moved = jnp.concatenate(link_rows(links, shift_recv[:, at].astype(F32)), axis=0)
            shift_recv[:, at] = moved.astype(BF16)

        for b in range(6):
            row = shift_recv[(b // 2) * 16 : (b // 2) * 16 + 16, :].astype(F32)
            row = row[(b % 2) * 8 : (b % 2) * 8 + 8]
            roll_v[b * 8 : b * 8 + 8] = rolled(inplane, row)

        @pl.loop(0, SITES // LANES)
        def _(t):
            at = pl.ds(t * LANES, LANES)
            links = links_v[inplane, :, at].astype(F32)
            moved = jnp.concatenate(link_rows(links, roll_v[:, at]), axis=0).astype(BF16)
            moved = jnp.where(z_first, moved, shift_recv[:, at]).astype(F32)
            cosines = cos_v[:, at]
            sines = sin_v[:, at]
            rows = []
            for a in range(3):
                re = moved[16 * a : 16 * a + 8]
                im = moved[16 * a + 8 : 16 * a + 16]
                rows += [cosines * re + sines * im, cosines * im - sines * re]
            phi_send[lax.rem(t, CHUNKS), lax.div(t, CHUNKS)] = jnp.concatenate(rows, axis=0).astype(BF16)

        for n in range(CHUNKS):
            for d, sem in ((2, phi_recv_sems.at[n]), (None, phi_recv_sems.at[n]), (1, phi_recv_sems.at[CHUNKS])):
                to_vec = near if d == 1 else (lax.rem(vec + 2, 4) if d == 2 else cross_core[1])
                pltpu.make_async_remote_copy(
                    src_ref=phi_send.at[n, to_vec], dst_ref=phi_recv.at[n, vec], send_sem=phi_send_sem.at[0],
                    recv_sem=sem, device_id=(space, to_vec), device_id_type=MESH,
                ).start()
        pltpu.make_async_copy(phi_send.at[:, vec], phi_recv.at[:, vec], own_sem.at[1]).start()

    @pl.loop(0, 2)
    def _(turn):
        pl.when(turn == last)(phase_own)

        @pl.when((turn == 0) & (flat != 15))
        def _():
            pltpu.make_async_copy(piece_low, piece_low, shift_sems.at[4]).wait()
            pltpu.make_async_remote_copy(
                src_ref=piece_low, dst_ref=shift_recv.at[:, pl.ds(pl.multiple_of(flat * LANES, LANES), LANES)],
                send_sem=shift_sems.at[5], recv_sem=shift_sems.at[1], device_id=(layer + 15, vec), device_id_type=MESH,
            ).start()

    pl.semaphore_wait(known_sems.at[2], 2)
    st_three = st_recv.at[pl.ds(0, 3)]
    own_st.wait()
    pltpu.make_async_copy(st_three, st_three, st_sems.at[1]).wait()

    @pl.loop(0, 4)
    def _(source):
        st_wide[source] = st_recv[source].astype(F32)

    @pl.loop(0, CHUNKS * 4)
    def _(turn):
        n = lax.div(turn, 4)
        source = lax.rem(turn, 4)
        at = pl.ds(n * LANES, LANES)
        right = [[st_wide[k, 48 + 8 * b : 56 + 8 * b, at] for b in range(6)] for k in range(4)]
        for j in range(8):
            left = [
                jnp.broadcast_to(st_wide[source, 8 * b + j : 8 * b + j + 1, at], (8, LANES)) for b in range(6)
            ]
            start = source * 256 + j * 32
            for a in range(3):
                b = 2 * ((a + 1) % 3)
                c = 2 * ((a + 2) % 3)
                reals = []
                imags = []
                for k in range(4):
                    rbr, rbi, rcr, rci = right[k][b], right[k][b + 1], right[k][c], right[k][c + 1]
                    lbr, lbi, lcr, lci = left[b], left[b + 1], left[c], left[c + 1]
                    reals.append(lbr * rcr - lbi * rci - (lcr * rbr - lci * rbi))
                    imags.append(lbr * rci + lbi * rcr - (lcr * rbi + lci * rbr))
                table[n, pl.ds(start, 32), 2 * a * LANES : (2 * a + 1) * LANES] = jnp.concatenate(
                    reals, axis=0
                ).astype(BF16)
                table[n, pl.ds(start, 32), (2 * a + 1) * LANES : (2 * a + 2) * LANES] = jnp.concatenate(
                    imags, axis=0
                ).astype(BF16)

    def product(n, whose):
        real_rows = []
        imag_rows = []
        for c in range(2):
            field = phi_recv[n, 2 * whose + c].astype(F32)
            reals = [field[16 * a : 16 * a + 8] for a in range(3)]
            imags = [field[16 * a + 8 : 16 * a + 16] for a in range(3)]
            real_rows.append(jnp.concatenate([x for a in range(3) for x in (reals[a], -imags[a])], axis=1))
            imag_rows.append(jnp.concatenate([x for a in range(3) for x in (imags[a], reals[a])], axis=1))
        rows = jnp.concatenate(real_rows + imag_rows, axis=0).astype(BF16)
        return lax.dot_general(rows, table[n], (((1,), (1,)), ((), ())), preferred_element_type=F32)

    def scatter(at, total):
        for part in range(2):
            for c in range(2):
                start = part * 16 + c * 8
                for tile in range(8):
                    e_send[at, c, part * 8 + tile] = total[start : start + 8, tile * LANES : (tile + 1) * LANES]
        for d in FLAT_ORDER:
            to_space, to_vec = flat_peer(d)
            pltpu.make_async_remote_copy(
                src_ref=e_send.at[at, lax.rem(to_vec, 2), lax.rem(to_space, 16)], dst_ref=e_recv.at[at, d - 1],
                send_sem=e_sems.at[2], recv_sem=e_sems.at[at], device_id=(to_space, to_vec), device_id_type=MESH,
            ).start()

    def gathered(at):
        pltpu.make_async_copy(e_recv.at[at], e_recv.at[at], e_sems.at[at]).wait()
        total = e_send[at, core, flat]
        for d in range(31):
            total = total + e_recv[at, d]
        return total

    def send_z(at, d):
        to_space, to_vec = z_peer(d)
        pltpu.make_async_remote_copy(
            src_ref=z_send.at[at], dst_ref=z_recv.at[zee], send_sem=z_sems.at[2],
            recv_sem=z_sems.at[at], device_id=(to_space, to_vec), device_id_type=MESH,
        ).start()

    phi_near = phi_recv.at[:, 0]
    pltpu.make_async_copy(phi_near, phi_near, own_sem.at[1]).wait()
    pltpu.make_async_copy(phi_near, phi_near, phi_recv_sems.at[CHUNKS]).wait()
    total = product(0, half)
    for n in range(1, CHUNKS):
        total = total + product(n, half)
    scatter(0, total)

    total = None
    for n in range(CHUNKS):
        phi_two = phi_recv.at[n, pl.ds(0, 2)]
        pltpu.make_async_copy(phi_two, phi_two, phi_recv_sems.at[n]).wait()
        term = product(n, 1 - half)
        total = term if total is None else total + term
    scatter(1, total)

    z_send[0] = gathered(0)
    z_recv[zee] = z_send[0]
    for step in range(1, 8):
        send_z(0, half * 8 + lax.rem(zlow + step, 8) - zee + 16)

    z_send[1] = gathered(1)
    for step in (0, 1, 7, 2, 6, 3, 5, 4):
        send_z(1, (1 - half) * 8 + lax.rem(zlow + step, 8) - zee + 16)

    z_same = z_recv.at[pl.ds(0, 7)]
    z_other = z_recv.at[pl.ds(0, 8)]
    pltpu.make_async_copy(z_same, z_same, z_sems.at[0]).wait()
    pltpu.make_async_copy(z_other, z_other, z_sems.at[1]).wait()
    whole = z_recv[0]
    for z in range(1, 16):
        whole = whole + z_recv[z]
    ag_recv[flat] = whole * (1.0 / math.sqrt(SITES * PLANES))

    for d in FLAT_ORDER:
        if d < 16:
            pltpu.make_async_remote_copy(
                src_ref=ag_recv.at[flat], dst_ref=ag_recv.at[flat], send_sem=ag_sems.at[0],
                recv_sem=ag_sems.at[1], device_id=flat_peer(d), device_id_type=MESH,
            ).start()

    ag_others = ag_recv.at[pl.ds(0, 15)]
    pltpu.make_async_copy(ag_others, ag_others, ag_sems.at[1]).wait()
    for part in range(2):
        for tile in range(8):
            out[part, :, tile * LANES : (tile + 1) * LANES] = ag_recv[part * 8 + tile]

    pltpu.make_async_copy(st_three, st_three, st_sems.at[0]).wait()
    @pl.when(flat != 0)
    def _():
        pltpu.make_async_copy(shift_recv, shift_recv, shift_sems.at[0]).wait()

    @pl.when(flat == 0)
    def _():
        pieces = shift_recv.at[:, pl.ds(0, 15 * LANES)]
        pltpu.make_async_copy(pieces, pieces, shift_sems.at[0]).wait()

    pltpu.make_async_copy(piece, piece, shift_sems.at[3]).wait()

    @pl.when(flat != 15)
    def _():
        pltpu.make_async_copy(piece_low, piece_low, shift_sems.at[5]).wait()

    phi_three = phi_recv.at[:, pl.ds(0, 3)]
    pltpu.make_async_copy(phi_three, phi_three, phi_send_sem.at[0]).wait()
    pltpu.make_async_copy(e_recv, e_recv, e_sems.at[2]).wait()
    pltpu.make_async_copy(z_same, z_same, z_sems.at[2]).wait()
    pltpu.make_async_copy(z_other, z_other, z_sems.at[2]).wait()
    pltpu.make_async_copy(ag_others, ag_others, ag_sems.at[0]).wait()


def shards(vectors, gauge_links, momentum, directions, blocks):
    nblk = vectors.shape[0]
    vec = vectors.transpose(0, 2, 3, 1, 4).reshape(nblk, 48, SITES)
    links = gauge_links.reshape(3, 18, SITES)
    return pl.pallas_call(
        kernel,
        name="elementals",
        out_shape=jax.ShapeDtypeStruct((2, 8, 1024), F32),
        in_specs=[pl.BlockSpec(memory_space=pl.ANY)] * 5,
        out_specs=pl.BlockSpec(memory_space=pltpu.VMEM),
        scratch_shapes=[
            pltpu.SMEM((3,), jnp.int32),
            pltpu.SMEM((2,), jnp.int32),
            pltpu.SMEM((3,), jnp.int32),
            pltpu.VMEM((nblk, 48, SITES), BF16),
            pltpu.VMEM((3, 18, SITES), BF16),
            pltpu.VMEM((4, 96, QUARTER), BF16),
            pltpu.VMEM((4, 96, QUARTER), BF16),
            pltpu.VMEM((4, 96, QUARTER), F32),
            pltpu.VMEM((48, SITES), F32),
            pltpu.VMEM((48, SITES), BF16),
            pltpu.VMEM((48, SITES), BF16),
            pltpu.VMEM((48, LANES), BF16),
            pltpu.VMEM((48, LANES), BF16),
            pltpu.VMEM((8, SITES), F32),
            pltpu.VMEM((8, SITES), F32),
            pltpu.VMEM((CHUNKS, 4, 48, LANES), BF16),
            pltpu.VMEM((CHUNKS, 4, 48, LANES), BF16),
            pltpu.VMEM((CHUNKS, 1024, 6 * LANES), BF16),
            pltpu.VMEM((2, 2, 16, 8, LANES), F32),
            pltpu.VMEM((2, 31, 8, LANES), F32),
            pltpu.VMEM((2, 8, LANES), F32),
            pltpu.VMEM((16, 8, LANES), F32),
            pltpu.VMEM((16, 8, LANES), F32),
            pltpu.SemaphoreType.DMA((5,)),
            pltpu.SemaphoreType.DMA((2,)),
            pltpu.SemaphoreType.DMA((6,)),
            pltpu.SemaphoreType.DMA((2,)),
            pltpu.SemaphoreType.DMA((1,)),
            pltpu.SemaphoreType.DMA((CHUNKS + 1,)),
            pltpu.SemaphoreType.DMA((3,)),
            pltpu.SemaphoreType.DMA((3,)),
            pltpu.SemaphoreType.DMA((2,)),
            pltpu.SemaphoreType.REGULAR((3,)),
        ],
        compiler_params=pltpu.CompilerParams(
            collective_id=1, has_side_effects=True, vmem_limit_bytes=63 * 2**20
        ),
    )(momentum, directions, blocks, vec, links)


def solution(mesh):
    in_specs = (P(None, "vec", None, "space", None), P(None, None, "space", None), P(), P(), P())
    out_specs = P(None, "vec", None)
    return jax.shard_map(shards, mesh=mesh, in_specs=in_specs, out_specs=out_specs, check_vma=False)
```

```python
import functools
import math

import jax
import jax.numpy as jnp
from jax import lax
from jax.experimental import pallas as pl
from jax.experimental.pallas import tpu as pltpu
from jax.sharding import PartitionSpec as P

LX = 32
LY = 64
SITES = LX * LY
PLANES = 128
TWO_PI = 2.0 * math.pi
MESH = pl.DeviceIdType.MESH
F32 = jnp.float32
BF16 = jnp.bfloat16
LANES = 128
QUARTER = SITES // 4
CHUNKS = QUARTER // LANES
HALF = QUARTER // 2
FLAT_ORDER = sorted(range(1, 32), key=lambda d: -(min(d // 4 % 4, 4 - d // 4 % 4) + min(d % 4, 4 - d % 4)))


def link_rows(links, field):
    out = []
    for c in range(3):
        real_part = None
        for b in range(3):
            at = (c * 3 + b) * 2
            lr = links[at : at + 1]
            li = links[at + 1 : at + 2]
            fr = field[16 * b : 16 * b + 8]
            fi = field[16 * b + 8 : 16 * b + 16]
            re = lr * fr - li * fi
            im = lr * fi + li * fr
            real_part, imag_part = (re, im) if real_part is None else (real_part + re, imag_part + im)
        out += [real_part, imag_part]
    return out


def rolled(direction, row):
    lane = lax.broadcasted_iota(jnp.int32, row.shape, 1)
    next_x = pltpu.roll(row, SITES - LY, 1)
    next_y = jnp.where(
        lax.rem(lane, LY) == LY - 1, pltpu.roll(row, LY - 1, 1), pltpu.roll(row, SITES - 1, 1)
    )
    return jnp.where(direction == 0, next_x, next_y)


def kernel(
    momentum_hbm, directions_hbm, blocks_hbm, vec_hbm, links_hbm, out,
    momentum, directions, blocks, vec_v, links_v, st_send, st_recv, st_wide, roll_v, shift_send, shift_recv, piece, piece_low, cos_v, sin_v,
    phi_send, phi_recv, table, e_send, e_recv, z_send, z_recv, ag_recv,
    load_sem, own_sem, shift_sems, st_sems, phi_send_sem, phi_recv_sems, e_sems, z_sems, ag_sems, known_sems,
):
    space = lax.axis_index("space")
    vec = lax.axis_index("vec")
    flat = lax.rem(space, 16)
    zlow = lax.div(space, 16)
    half = lax.div(vec, 2)
    core = lax.rem(vec, 2)
    zee = half * 8 + zlow

    def flat_peer(d):
        x = lax.rem(lax.div(flat, 4) + lax.rem(lax.div(d, 4), 4), 4)
        y = lax.rem(flat + lax.rem(d, 4), 4)
        return zlow * 16 + x * 4 + y, half * 2 + lax.rem(core + lax.div(d, 16), 2)

    def z_peer(d):
        z = lax.rem(zee + d, 16)
        return lax.rem(z, 8) * 16 + flat, lax.div(z, 8) * 2 + core

    def vec_peer(d):
        return space, lax.rem(vec + d, 4)

    layer = zlow * 16
    up = (lax.rem(zlow + 1, 8) * 16 + flat, vec)
    down = (lax.rem(zlow + 7, 8) * 16 + flat, vec)
    last = lax.div(flat, 15)
    near = half * 2 + (1 - core)
    cross_core = (space, (1 - half) * 2 + (1 - core))

    barrier = pltpu.get_barrier_semaphore()

    def greet(device):
        pl.semaphore_signal(barrier, inc=1, device_id=device, device_id_type=MESH)

    greet(z_peer(8))
    greet(cross_core)
    greet(z_peer(1))
    greet(z_peer(15))
    greet(up)

    @pl.loop(1, 32)
    def _(d):
        greet(flat_peer(d))

    loads = [
        pltpu.make_async_copy(source, target, load_sem.at[at])
        for at, (source, target) in enumerate(
            (
                (blocks_hbm, blocks), (vec_hbm, vec_v), (links_hbm, links_v),
                (directions_hbm, directions), (momentum_hbm, momentum),
            )
        )
    ]
    for load in loads:
        load.start()
    for load in loads:
        load.wait()

    def pass_on(at, steps):
        for d in (steps, 16 - steps):
            pl.semaphore_signal(known_sems.at[at], inc=1, device_id=z_peer(d), device_id_type=MESH)

    first_step = directions[0]
    z_first = first_step == 2
    inplane = jnp.where(z_first, directions[1], first_step)

    for q in range(4):
        for part in range(2):
            at = slice(q * QUARTER + part * HALF, q * QUARTER + (part + 1) * HALF)
            st_send[part, q, 0:48] = vec_v[blocks[1], :, at]
            st_send[part, q, 48:96] = vec_v[blocks[2], :, at]

    for b in range(6):
        row = vec_v[blocks[0], (b // 2) * 16 : (b // 2) * 16 + 16, :].astype(F32)
        row = row[(b % 2) * 8 : (b % 2) * 8 + 8]
        roll_v[b * 8 : b * 8 + 8] = rolled(inplane, row)

    @pl.loop(0, SITES // 256)
    def _(t):
        at = pl.ds(t * 256, 256)
        links = links_v[inplane, :, at].astype(F32)
        moved = jnp.concatenate(link_rows(links, roll_v[:, at]), axis=0).astype(BF16)
        shift_send[:, at] = jnp.where(z_first, vec_v[blocks[0], :, at], moved)

    pl.semaphore_wait(barrier, 31 + 5)

    @pl.when(flat != 0)
    def _():
        pltpu.make_async_remote_copy(
            src_ref=shift_send, dst_ref=shift_recv, send_sem=shift_sems.at[0], recv_sem=shift_sems.at[1],
            device_id=(space - 1, vec), device_id_type=MESH,
        ).start()

    @pl.when(flat == 0)
    def _():
        pltpu.make_async_copy(shift_send.at[:, pl.ds(0, LANES)], piece, shift_sems.at[2]).start()
        for k in range(15, 0, -1):
            pltpu.make_async_remote_copy(
                src_ref=shift_send.at[:, pl.ds(k * LANES, LANES)], dst_ref=piece, send_sem=shift_sems.at[0],
                recv_sem=shift_sems.at[2], device_id=(layer + k, vec), device_id_type=MESH,
            ).start()

    def exchange(part):
        for d in (2, 1, 3):
            target = lax.rem(vec + d, 4)
            pltpu.make_async_remote_copy(
                src_ref=st_send.at[part, target], dst_ref=st_recv.at[part, vec], send_sem=st_sems.at[2],
                recv_sem=st_sems.at[part], device_id=vec_peer(d), device_id_type=MESH,
            ).start()
        pltpu.make_async_copy(st_send.at[part, vec], st_recv.at[part, vec], own_sem.at[part]).start()

    exchange(0)
    pass_on(0, 1)
    pl.semaphore_wait(known_sems.at[0], 2)
    pass_on(1, 2)
    site = lax.broadcasted_iota(jnp.int32, (8, SITES), 1)
    fraction = ((momentum[0] * lax.div(site, LY)) & (LX - 1)).astype(F32) / LX
    fraction = fraction + ((momentum[1] * lax.rem(site, LY)) & (LY - 1)).astype(F32) / LY
    fraction = fraction + ((momentum[2] * space) & (PLANES - 1)).astype(F32) / PLANES
    angles = TWO_PI * fraction
    cos_v[...] = jnp.cos(angles)
    sin_v[...] = jnp.sin(angles)

    pltpu.make_async_copy(piece, piece, shift_sems.at[2]).wait()

    def forward(dst, sem):
        pltpu.make_async_remote_copy(
            src_ref=piece, dst_ref=dst, send_sem=shift_sems.at[3], recv_sem=sem, device_id=down, device_id_type=MESH,
        ).start()

    @pl.when(flat != 15)
    def _():
        forward(piece_low, shift_sems.at[4])

    @pl.when(flat == 15)
    def _():
        forward(shift_recv.at[:, pl.ds(15 * LANES, LANES)], shift_sems.at[1])

    exchange(1)
    pl.semaphore_wait(known_sems.at[1], 2)
    pass_on(2, 4)

    def phase_own():
        pltpu.make_async_copy(shift_recv, shift_recv, shift_sems.at[1]).wait()

        @pl.loop(0, SITES // 256)
        def _(t):
            at = pl.ds(t * 256, 256)
            links = links_v[2, :, at].astype(F32)
            moved = jnp.concatenate(link_rows(links, shift_recv[:, at].astype(F32)), axis=0)
            shift_recv[:, at] = moved.astype(BF16)

        for b in range(6):
            row = shift_recv[(b // 2) * 16 : (b // 2) * 16 + 16, :].astype(F32)
            row = row[(b % 2) * 8 : (b % 2) * 8 + 8]
            roll_v[b * 8 : b * 8 + 8] = rolled(inplane, row)

        @pl.loop(0, SITES // LANES)
        def _(t):
            at = pl.ds(t * LANES, LANES)
            links = links_v[inplane, :, at].astype(F32)
            moved = jnp.concatenate(link_rows(links, roll_v[:, at]), axis=0).astype(BF16)
            moved = jnp.where(z_first, moved, shift_recv[:, at]).astype(F32)
            cosines = cos_v[:, at]
            sines = sin_v[:, at]
            rows = []
            for a in range(3):
                re = moved[16 * a : 16 * a + 8]
                im = moved[16 * a + 8 : 16 * a + 16]
                rows += [cosines * re + sines * im, cosines * im - sines * re]
            phi_send[lax.rem(t, CHUNKS), lax.div(t, CHUNKS)] = jnp.concatenate(rows, axis=0).astype(BF16)

        pltpu.make_async_copy(phi_send.at[:, vec], phi_recv.at[:, vec], own_sem.at[2]).start()
        pltpu.make_async_remote_copy(
            src_ref=phi_send.at[:, near], dst_ref=phi_recv.at[:, vec], send_sem=phi_send_sem.at[0],
            recv_sem=phi_recv_sems.at[CHUNKS], device_id=(space, near), device_id_type=MESH,
        ).start()

    @pl.loop(0, 2)
    def _(turn):
        pl.when(turn == last)(phase_own)

        @pl.when((turn == 0) & (flat != 15))
        def _():
            pltpu.make_async_copy(piece_low, piece_low, shift_sems.at[4]).wait()
            pltpu.make_async_remote_copy(
                src_ref=piece_low, dst_ref=shift_recv.at[:, pl.ds(pl.multiple_of(flat * LANES, LANES), LANES)],
                send_sem=shift_sems.at[5], recv_sem=shift_sems.at[1], device_id=(layer + 15, vec), device_id_type=MESH,
            ).start()

    pl.semaphore_wait(known_sems.at[2], 2)
    def send_far():
        for n in range(CHUNKS):
            for to_vec in (lax.rem(vec + 2, 4), cross_core[1]):
                pltpu.make_async_remote_copy(
                    src_ref=phi_send.at[n, to_vec], dst_ref=phi_recv.at[n, vec], send_sem=phi_send_sem.at[0],
                    recv_sem=phi_recv_sems.at[n], device_id=(space, to_vec), device_id_type=MESH,
                ).start()

    st_three = st_recv.at[0, pl.ds(0, 3)]

    def make_table(part):
        own_st = st_recv.at[part, 0]
        pltpu.make_async_copy(own_st, own_st, own_sem.at[part]).wait()
        pltpu.make_async_copy(st_three, st_three, st_sems.at[part]).wait()

        @pl.loop(0, 4)
        def _(source):
            st_wide[source] = st_recv[part, source].astype(F32)

        @pl.loop(0, 8)
        def _(turn):
            n = part * 2 + lax.div(turn, 4)
            source = lax.rem(turn, 4)
            at = pl.ds(lax.div(turn, 4) * LANES, LANES)
            right = [[st_wide[k, 48 + 8 * b : 56 + 8 * b, at] for b in range(6)] for k in range(4)]
            for j in range(8):
                left = [
                    jnp.broadcast_to(st_wide[source, 8 * b + j : 8 * b + j + 1, at], (8, LANES)) for b in range(6)
                ]
                start = source * 256 + j * 32
                for a in range(3):
                    b = 2 * ((a + 1) % 3)
                    c = 2 * ((a + 2) % 3)
                    reals = []
                    imags = []
                    for k in range(4):
                        rbr, rbi, rcr, rci = right[k][b], right[k][b + 1], right[k][c], right[k][c + 1]
                        lbr, lbi, lcr, lci = left[b], left[b + 1], left[c], left[c + 1]
                        reals.append(lbr * rcr - lbi * rci - (lcr * rbr - lci * rbi))
                        imags.append(lbr * rci + lbi * rcr - (lcr * rbi + lci * rbr))
                    table[n, pl.ds(start, 32), 2 * a * LANES : (2 * a + 1) * LANES] = jnp.concatenate(
                        reals, axis=0
                    ).astype(BF16)
                    table[n, pl.ds(start, 32), (2 * a + 1) * LANES : (2 * a + 2) * LANES] = jnp.concatenate(
                        imags, axis=0
                    ).astype(BF16)

    def product(n, whose):
        real_rows = []
        imag_rows = []
        for c in range(2):
            field = phi_recv[n, 2 * whose + c].astype(F32)
            reals = [field[16 * a : 16 * a + 8] for a in range(3)]
            imags = [field[16 * a + 8 : 16 * a + 16] for a in range(3)]
            real_rows.append(jnp.concatenate([x for a in range(3) for x in (reals[a], -imags[a])], axis=1))
            imag_rows.append(jnp.concatenate([x for a in range(3) for x in (imags[a], reals[a])], axis=1))
        rows = jnp.concatenate(real_rows + imag_rows, axis=0).astype(BF16)
        return lax.dot_general(rows, table[n], (((1,), (1,)), ((), ())), preferred_element_type=F32)

    def scatter(at, total):
        for part in range(2):
            for c in range(2):
                start = part * 16 + c * 8
                for tile in range(8):
                    e_send[at, c, part * 8 + tile] = total[start : start + 8, tile * LANES : (tile + 1) * LANES]
        for d in FLAT_ORDER:
            to_space, to_vec = flat_peer(d)
            pltpu.make_async_remote_copy(
                src_ref=e_send.at[at, lax.rem(to_vec, 2), lax.rem(to_space, 16)], dst_ref=e_recv.at[at, d - 1],
                send_sem=e_sems.at[2], recv_sem=e_sems.at[at], device_id=(to_space, to_vec), device_id_type=MESH,
            ).start()

    def gathered(at):
        pltpu.make_async_copy(e_recv.at[at], e_recv.at[at], e_sems.at[at]).wait()
        total = e_send[at, core, flat]
        for d in range(31):
            total = total + e_recv[at, d]
        return total

    def send_z(at, d):
        to_space, to_vec = z_peer(d)
        pltpu.make_async_remote_copy(
            src_ref=z_send.at[at], dst_ref=z_recv.at[zee], send_sem=z_sems.at[2],
            recv_sem=z_sems.at[at], device_id=(to_space, to_vec), device_id_type=MESH,
        ).start()

    make_table(0)
    phi_near = phi_recv.at[:, 0]
    pltpu.make_async_copy(phi_near, phi_near, own_sem.at[2]).wait()
    pltpu.make_async_copy(phi_near, phi_near, phi_recv_sems.at[CHUNKS]).wait()
    total = product(0, half) + product(1, half)
    for part in range(2):
        pltpu.make_async_copy(st_three, st_three, st_sems.at[2]).wait()
    send_far()
    make_table(1)
    total = total + product(2, half) + product(3, half)
    scatter(0, total)

    total = None
    for n in range(CHUNKS):
        phi_two = phi_recv.at[n, pl.ds(0, 2)]
        pltpu.make_async_copy(phi_two, phi_two, phi_recv_sems.at[n]).wait()
        term = product(n, 1 - half)
        total = term if total is None else total + term
    scatter(1, total)

    z_send[0] = gathered(0)
    z_recv[zee] = z_send[0]
    for step in range(1, 8):
        send_z(0, half * 8 + lax.rem(zlow + step, 8) - zee + 16)

    z_send[1] = gathered(1)
    for step in (0, 1, 7, 2, 6, 3, 5, 4):
        send_z(1, (1 - half) * 8 + lax.rem(zlow + step, 8) - zee + 16)

    z_same = z_recv.at[pl.ds(0, 7)]
    z_other = z_recv.at[pl.ds(0, 8)]
    pltpu.make_async_copy(z_same, z_same, z_sems.at[0]).wait()
    pltpu.make_async_copy(z_other, z_other, z_sems.at[1]).wait()
    whole = z_recv[0]
    for z in range(1, 16):
        whole = whole + z_recv[z]
    ag_recv[flat] = whole * (1.0 / math.sqrt(SITES * PLANES))

    for d in FLAT_ORDER:
        if d < 16:
            pltpu.make_async_remote_copy(
                src_ref=ag_recv.at[flat], dst_ref=ag_recv.at[flat], send_sem=ag_sems.at[0],
                recv_sem=ag_sems.at[1], device_id=flat_peer(d), device_id_type=MESH,
            ).start()

    ag_others = ag_recv.at[pl.ds(0, 15)]
    pltpu.make_async_copy(ag_others, ag_others, ag_sems.at[1]).wait()
    for part in range(2):
        for tile in range(8):
            out[part, :, tile * LANES : (tile + 1) * LANES] = ag_recv[part * 8 + tile]

    @pl.when(flat != 0)
    def _():
        pltpu.make_async_copy(shift_recv, shift_recv, shift_sems.at[0]).wait()

    @pl.when(flat == 0)
    def _():
        pieces = shift_recv.at[:, pl.ds(0, 15 * LANES)]
        pltpu.make_async_copy(pieces, pieces, shift_sems.at[0]).wait()

    pltpu.make_async_copy(piece, piece, shift_sems.at[3]).wait()

    @pl.when(flat != 15)
    def _():
        pltpu.make_async_copy(piece_low, piece_low, shift_sems.at[5]).wait()

    phi_three = phi_recv.at[:, pl.ds(0, 3)]
    pltpu.make_async_copy(phi_three, phi_three, phi_send_sem.at[0]).wait()
    pltpu.make_async_copy(e_recv, e_recv, e_sems.at[2]).wait()
    pltpu.make_async_copy(z_same, z_same, z_sems.at[2]).wait()
    pltpu.make_async_copy(z_other, z_other, z_sems.at[2]).wait()
    pltpu.make_async_copy(ag_others, ag_others, ag_sems.at[0]).wait()


def shards(vectors, gauge_links, momentum, directions, blocks):
    nblk = vectors.shape[0]
    vec = vectors.transpose(0, 2, 3, 1, 4).reshape(nblk, 48, SITES)
    links = gauge_links.reshape(3, 18, SITES)
    return pl.pallas_call(
        kernel,
        name="elementals",
        out_shape=jax.ShapeDtypeStruct((2, 8, 1024), F32),
        in_specs=[pl.BlockSpec(memory_space=pl.ANY)] * 5,
        out_specs=pl.BlockSpec(memory_space=pltpu.VMEM),
        scratch_shapes=[
            pltpu.SMEM((3,), jnp.int32),
            pltpu.SMEM((2,), jnp.int32),
            pltpu.SMEM((3,), jnp.int32),
            pltpu.VMEM((nblk, 48, SITES), BF16),
            pltpu.VMEM((3, 18, SITES), BF16),
            pltpu.VMEM((2, 4, 96, HALF), BF16),
            pltpu.VMEM((2, 4, 96, HALF), BF16),
            pltpu.VMEM((4, 96, HALF), F32),
            pltpu.VMEM((48, SITES), F32),
            pltpu.VMEM((48, SITES), BF16),
            pltpu.VMEM((48, SITES), BF16),
            pltpu.VMEM((48, LANES), BF16),
            pltpu.VMEM((48, LANES), BF16),
            pltpu.VMEM((8, SITES), F32),
            pltpu.VMEM((8, SITES), F32),
            pltpu.VMEM((CHUNKS, 4, 48, LANES), BF16),
            pltpu.VMEM((CHUNKS, 4, 48, LANES), BF16),
            pltpu.VMEM((CHUNKS, 1024, 6 * LANES), BF16),
            pltpu.VMEM((2, 2, 16, 8, LANES), F32),
            pltpu.VMEM((2, 31, 8, LANES), F32),
            pltpu.VMEM((2, 8, LANES), F32),
            pltpu.VMEM((16, 8, LANES), F32),
            pltpu.VMEM((16, 8, LANES), F32),
            pltpu.SemaphoreType.DMA((5,)),
            pltpu.SemaphoreType.DMA((3,)),
            pltpu.SemaphoreType.DMA((6,)),
            pltpu.SemaphoreType.DMA((3,)),
            pltpu.SemaphoreType.DMA((1,)),
            pltpu.SemaphoreType.DMA((CHUNKS + 1,)),
            pltpu.SemaphoreType.DMA((3,)),
            pltpu.SemaphoreType.DMA((3,)),
            pltpu.SemaphoreType.DMA((2,)),
            pltpu.SemaphoreType.REGULAR((3,)),
        ],
        compiler_params=pltpu.CompilerParams(
            collective_id=1, has_side_effects=True, vmem_limit_bytes=63 * 2**20
        ),
    )(momentum, directions, blocks, vec, links)


def solution(mesh):
    in_specs = (P(None, "vec", None, "space", None), P(None, None, "space", None), P(), P(), P())
    out_specs = P(None, "vec", None)
    return jax.shard_map(shards, mesh=mesh, in_specs=in_specs, out_specs=out_specs, check_vma=False)
```

```python
import functools
import math

import jax
import jax.numpy as jnp
from jax import lax
from jax.experimental import pallas as pl
from jax.experimental.pallas import tpu as pltpu
from jax.sharding import PartitionSpec as P

LX = 32
LY = 64
SITES = LX * LY
PLANES = 128
TWO_PI = 2.0 * math.pi
MESH = pl.DeviceIdType.MESH
F32 = jnp.float32
BF16 = jnp.bfloat16
LANES = 128
QUARTER = SITES // 4
CHUNKS = QUARTER // LANES
HALF = QUARTER // 2
FLAT_ORDER = sorted(range(1, 32), key=lambda d: -(min(d // 4 % 4, 4 - d // 4 % 4) + min(d % 4, 4 - d % 4)))


def link_rows(links, field):
    out = []
    for c in range(3):
        real_part = None
        for b in range(3):
            at = (c * 3 + b) * 2
            lr = links[at : at + 1]
            li = links[at + 1 : at + 2]
            fr = field[16 * b : 16 * b + 8]
            fi = field[16 * b + 8 : 16 * b + 16]
            re = lr * fr - li * fi
            im = lr * fi + li * fr
            real_part, imag_part = (re, im) if real_part is None else (real_part + re, imag_part + im)
        out += [real_part, imag_part]
    return out


def rolled(direction, row):
    lane = lax.broadcasted_iota(jnp.int32, row.shape, 1)
    next_x = pltpu.roll(row, SITES - LY, 1)
    next_y = jnp.where(
        lax.rem(lane, LY) == LY - 1, pltpu.roll(row, LY - 1, 1), pltpu.roll(row, SITES - 1, 1)
    )
    return jnp.where(direction == 0, next_x, next_y)


def kernel(
    momentum_hbm, directions_hbm, blocks_hbm, vec_hbm, links_hbm, out,
    momentum, directions, blocks, vec_v, links_v, st_send, st_recv, st_wide, roll_v, shift_send, shift_recv, piece, piece_low, cos_v, sin_v,
    phi_send, phi_recv, table, e_send, e_recv, z_send, z_recv, mine,
    load_sem, own_sem, shift_sems, st_sems, phi_send_sem, phi_recv_sems, e_sems, z_sems, ag_sems, known_sems,
):
    space = lax.axis_index("space")
    vec = lax.axis_index("vec")
    flat = lax.rem(space, 16)
    zlow = lax.div(space, 16)
    half = lax.div(vec, 2)
    core = lax.rem(vec, 2)
    zee = half * 8 + zlow

    def flat_peer(d):
        x = lax.rem(lax.div(flat, 4) + lax.rem(lax.div(d, 4), 4), 4)
        y = lax.rem(flat + lax.rem(d, 4), 4)
        return zlow * 16 + x * 4 + y, half * 2 + lax.rem(core + lax.div(d, 16), 2)

    def z_peer(d):
        z = lax.rem(zee + d, 16)
        return lax.rem(z, 8) * 16 + flat, lax.div(z, 8) * 2 + core

    def vec_peer(d):
        return space, lax.rem(vec + d, 4)

    layer = zlow * 16
    up = (lax.rem(zlow + 1, 8) * 16 + flat, vec)
    down = (lax.rem(zlow + 7, 8) * 16 + flat, vec)
    last = lax.div(flat, 15)
    near = half * 2 + (1 - core)
    cross_core = (space, (1 - half) * 2 + (1 - core))

    barrier = pltpu.get_barrier_semaphore()

    def greet(device):
        pl.semaphore_signal(barrier, inc=1, device_id=device, device_id_type=MESH)

    greet(z_peer(8))
    greet(cross_core)
    greet(z_peer(1))
    greet(z_peer(15))
    greet(up)

    @pl.loop(1, 32)
    def _(d):
        greet(flat_peer(d))

    loads = [
        pltpu.make_async_copy(source, target, load_sem.at[at])
        for at, (source, target) in enumerate(
            (
                (blocks_hbm, blocks), (vec_hbm, vec_v), (links_hbm, links_v),
                (directions_hbm, directions), (momentum_hbm, momentum),
            )
        )
    ]
    for load in loads:
        load.start()
    for load in loads:
        load.wait()

    def pass_on(at, steps):
        for d in (steps, 16 - steps):
            pl.semaphore_signal(known_sems.at[at], inc=1, device_id=z_peer(d), device_id_type=MESH)

    first_step = directions[0]
    z_first = first_step == 2
    inplane = jnp.where(z_first, directions[1], first_step)

    for q in range(4):
        for part in range(2):
            at = slice(q * QUARTER + part * HALF, q * QUARTER + (part + 1) * HALF)
            st_send[part, q, 0:48] = vec_v[blocks[1], :, at]
            st_send[part, q, 48:96] = vec_v[blocks[2], :, at]

    for b in range(6):
        row = vec_v[blocks[0], (b // 2) * 16 : (b // 2) * 16 + 16, :].astype(F32)
        row = row[(b % 2) * 8 : (b % 2) * 8 + 8]
        roll_v[b * 8 : b * 8 + 8] = rolled(inplane, row)

    @pl.loop(0, SITES // 256)
    def _(t):
        at = pl.ds(t * 256, 256)
        links = links_v[inplane, :, at].astype(F32)
        moved = jnp.concatenate(link_rows(links, roll_v[:, at]), axis=0).astype(BF16)
        shift_send[:, at] = jnp.where(z_first, vec_v[blocks[0], :, at], moved)

    pl.semaphore_wait(barrier, 31 + 5)

    @pl.when(flat != 0)
    def _():
        pltpu.make_async_remote_copy(
            src_ref=shift_send, dst_ref=shift_recv, send_sem=shift_sems.at[0], recv_sem=shift_sems.at[1],
            device_id=(space - 1, vec), device_id_type=MESH,
        ).start()

    @pl.when(flat == 0)
    def _():
        pltpu.make_async_copy(shift_send.at[:, pl.ds(0, LANES)], piece, shift_sems.at[2]).start()
        for k in range(15, 0, -1):
            pltpu.make_async_remote_copy(
                src_ref=shift_send.at[:, pl.ds(k * LANES, LANES)], dst_ref=piece, send_sem=shift_sems.at[0],
                recv_sem=shift_sems.at[2], device_id=(layer + k, vec), device_id_type=MESH,
            ).start()

    def exchange(part, steps):
        for d in steps:
            target = lax.rem(vec + d, 4)
            pltpu.make_async_remote_copy(
                src_ref=st_send.at[part, target], dst_ref=st_recv.at[part, vec], send_sem=st_sems.at[2],
                recv_sem=st_sems.at[part], device_id=vec_peer(d), device_id_type=MESH,
            ).start()

    exchange(0, (2, 1))
    for part in range(2):
        pltpu.make_async_copy(st_send.at[part, vec], st_recv.at[part, vec], own_sem.at[part]).start()
    pass_on(0, 1)
    pl.semaphore_wait(known_sems.at[0], 2)
    pass_on(1, 2)
    site = lax.broadcasted_iota(jnp.int32, (8, SITES), 1)
    fraction = ((momentum[0] * lax.div(site, LY)) & (LX - 1)).astype(F32) / LX
    fraction = fraction + ((momentum[1] * lax.rem(site, LY)) & (LY - 1)).astype(F32) / LY
    fraction = fraction + ((momentum[2] * space) & (PLANES - 1)).astype(F32) / PLANES
    angles = TWO_PI * fraction
    cos_v[...] = jnp.cos(angles)
    sin_v[...] = jnp.sin(angles)

    pltpu.make_async_copy(piece, piece, shift_sems.at[2]).wait()

    def forward(dst, sem):
        pltpu.make_async_remote_copy(
            src_ref=piece, dst_ref=dst, send_sem=shift_sems.at[3], recv_sem=sem, device_id=down, device_id_type=MESH,
        ).start()

    @pl.when(flat != 15)
    def _():
        forward(piece_low, shift_sems.at[4])

    @pl.when(flat == 15)
    def _():
        forward(shift_recv.at[:, pl.ds(15 * LANES, LANES)], shift_sems.at[1])

    exchange(0, (3,))
    exchange(1, (2, 3, 1))
    pl.semaphore_wait(known_sems.at[1], 2)
    pass_on(2, 4)

    def phase_own():
        pltpu.make_async_copy(shift_recv, shift_recv, shift_sems.at[1]).wait()

        @pl.loop(0, SITES // 256)
        def _(t):
            at = pl.ds(t * 256, 256)
            links = links_v[2, :, at].astype(F32)
            moved = jnp.concatenate(link_rows(links, shift_recv[:, at].astype(F32)), axis=0)
            shift_recv[:, at] = moved.astype(BF16)

        for b in range(6):
            row = shift_recv[(b // 2) * 16 : (b // 2) * 16 + 16, :].astype(F32)
            row = row[(b % 2) * 8 : (b % 2) * 8 + 8]
            roll_v[b * 8 : b * 8 + 8] = rolled(inplane, row)

        @pl.loop(0, SITES // LANES)
        def _(t):
            at = pl.ds(t * LANES, LANES)
            links = links_v[inplane, :, at].astype(F32)
            moved = jnp.concatenate(link_rows(links, roll_v[:, at]), axis=0).astype(BF16)
            moved = jnp.where(z_first, moved, shift_recv[:, at]).astype(F32)
            cosines = cos_v[:, at]
            sines = sin_v[:, at]
            rows = []
            for a in range(3):
                re = moved[16 * a : 16 * a + 8]
                im = moved[16 * a + 8 : 16 * a + 16]
                rows += [cosines * re + sines * im, cosines * im - sines * re]
            phi_send[lax.rem(t, CHUNKS), lax.div(t, CHUNKS)] = jnp.concatenate(rows, axis=0).astype(BF16)

        pltpu.make_async_copy(phi_send.at[:, vec], phi_recv.at[:, vec], own_sem.at[2]).start()
        pltpu.make_async_remote_copy(
            src_ref=phi_send.at[:, near], dst_ref=phi_recv.at[:, vec], send_sem=phi_send_sem.at[0],
            recv_sem=phi_recv_sems.at[CHUNKS], device_id=(space, near), device_id_type=MESH,
        ).start()

    @pl.loop(0, 2)
    def _(turn):
        pl.when(turn == last)(phase_own)

        @pl.when((turn == 0) & (flat != 15))
        def _():
            pltpu.make_async_copy(piece_low, piece_low, shift_sems.at[4]).wait()
            pltpu.make_async_remote_copy(
                src_ref=piece_low, dst_ref=shift_recv.at[:, pl.ds(pl.multiple_of(flat * LANES, LANES), LANES)],
                send_sem=shift_sems.at[5], recv_sem=shift_sems.at[1], device_id=(layer + 15, vec), device_id_type=MESH,
            ).start()

    pl.semaphore_wait(known_sems.at[2], 2)
    def send_far():
        for n in range(CHUNKS):
            for to_vec in (lax.rem(vec + 2, 4), cross_core[1]):
                pltpu.make_async_remote_copy(
                    src_ref=phi_send.at[n, to_vec], dst_ref=phi_recv.at[n, vec], send_sem=phi_send_sem.at[0],
                    recv_sem=phi_recv_sems.at[n], device_id=(space, to_vec), device_id_type=MESH,
                ).start()

    st_three = st_recv.at[0, pl.ds(0, 3)]

    def make_table(part):
        own_st = st_recv.at[part, 0]
        pltpu.make_async_copy(own_st, own_st, own_sem.at[part]).wait()
        pltpu.make_async_copy(st_three, st_three, st_sems.at[part]).wait()

        @pl.loop(0, 4)
        def _(source):
            st_wide[source] = st_recv[part, source].astype(F32)

        @pl.loop(0, 8)
        def _(turn):
            n = part * 2 + lax.div(turn, 4)
            source = lax.rem(turn, 4)
            at = pl.ds(lax.div(turn, 4) * LANES, LANES)
            right = [[st_wide[k, 48 + 8 * b : 56 + 8 * b, at] for b in range(6)] for k in range(4)]
            for j in range(8):
                left = [
                    jnp.broadcast_to(st_wide[source, 8 * b + j : 8 * b + j + 1, at], (8, LANES)) for b in range(6)
                ]
                start = source * 256 + j * 32
                for a in range(3):
                    b = 2 * ((a + 1) % 3)
                    c = 2 * ((a + 2) % 3)
                    reals = []
                    imags = []
                    for k in range(4):
                        rbr, rbi, rcr, rci = right[k][b], right[k][b + 1], right[k][c], right[k][c + 1]
                        lbr, lbi, lcr, lci = left[b], left[b + 1], left[c], left[c + 1]
                        reals.append(lbr * rcr - lbi * rci - (lcr * rbr - lci * rbi))
                        imags.append(lbr * rci + lbi * rcr - (lcr * rbi + lci * rbr))
                    table[n, pl.ds(start, 32), 2 * a * LANES : (2 * a + 1) * LANES] = jnp.concatenate(
                        reals, axis=0
                    ).astype(BF16)
                    table[n, pl.ds(start, 32), (2 * a + 1) * LANES : (2 * a + 2) * LANES] = jnp.concatenate(
                        imags, axis=0
                    ).astype(BF16)

    def product(n, whose):
        real_rows = []
        imag_rows = []
        for c in range(2):
            field = phi_recv[n, 2 * whose + c].astype(F32)
            reals = [field[16 * a : 16 * a + 8] for a in range(3)]
            imags = [field[16 * a + 8 : 16 * a + 16] for a in range(3)]
            real_rows.append(jnp.concatenate([x for a in range(3) for x in (reals[a], -imags[a])], axis=1))
            imag_rows.append(jnp.concatenate([x for a in range(3) for x in (imags[a], reals[a])], axis=1))
        rows = jnp.concatenate(real_rows + imag_rows, axis=0).astype(BF16)
        return lax.dot_general(rows, table[n], (((1,), (1,)), ((), ())), preferred_element_type=F32)

    def scatter(at, total):
        for part in range(2):
            for c in range(2):
                start = part * 16 + c * 8
                for tile in range(8):
                    e_send[at, c, part * 8 + tile] = total[start : start + 8, tile * LANES : (tile + 1) * LANES]
        for d in FLAT_ORDER:
            to_space, to_vec = flat_peer(d)
            pltpu.make_async_remote_copy(
                src_ref=e_send.at[at, lax.rem(to_vec, 2), lax.rem(to_space, 16)], dst_ref=e_recv.at[at, d - 1],
                send_sem=e_sems.at[2], recv_sem=e_sems.at[at], device_id=(to_space, to_vec), device_id_type=MESH,
            ).start()

    def gathered(at):
        pltpu.make_async_copy(e_recv.at[at], e_recv.at[at], e_sems.at[at]).wait()
        total = e_send[at, core, flat]
        for d in range(31):
            total = total + e_recv[at, d]
        return total

    def send_z(at, d):
        to_space, to_vec = z_peer(d)
        pltpu.make_async_remote_copy(
            src_ref=z_send.at[at], dst_ref=z_recv.at[zee], send_sem=z_sems.at[2],
            recv_sem=z_sems.at[at], device_id=(to_space, to_vec), device_id_type=MESH,
        ).start()

    make_table(0)
    phi_near = phi_recv.at[:, 0]
    pltpu.make_async_copy(phi_near, phi_near, own_sem.at[2]).wait()
    pltpu.make_async_copy(phi_near, phi_near, phi_recv_sems.at[CHUNKS]).wait()
    total = product(0, half) + product(1, half)
    for part in range(2):
        pltpu.make_async_copy(st_three, st_three, st_sems.at[2]).wait()
    send_far()
    make_table(1)
    total = total + product(2, half) + product(3, half)
    scatter(0, total)

    total = None
    for n in range(CHUNKS):
        phi_two = phi_recv.at[n, pl.ds(0, 2)]
        pltpu.make_async_copy(phi_two, phi_two, phi_recv_sems.at[n]).wait()
        term = product(n, 1 - half)
        total = term if total is None else total + term
    scatter(1, total)

    z_send[0] = gathered(0)
    z_recv[zee] = z_send[0]
    for step in range(1, 8):
        send_z(0, half * 8 + lax.rem(zlow + step, 8) - zee + 16)

    z_send[1] = gathered(1)
    for step in (0, 1, 7, 2, 6, 3, 5, 4):
        send_z(1, (1 - half) * 8 + lax.rem(zlow + step, 8) - zee + 16)

    z_same = z_recv.at[pl.ds(0, 7)]
    z_other = z_recv.at[pl.ds(0, 8)]
    pltpu.make_async_copy(z_same, z_same, z_sems.at[0]).wait()
    pltpu.make_async_copy(z_other, z_other, z_sems.at[1]).wait()
    whole = z_recv[0]
    for z in range(1, 16):
        whole = whole + z_recv[z]
    mine[...] = whole * (1.0 / math.sqrt(SITES * PLANES))
    place = out.at[lax.div(flat, 8), :, pl.ds(pl.multiple_of(lax.rem(flat, 8) * LANES, LANES), LANES)]
    own_out = pltpu.make_async_copy(mine, place, load_sem.at[0])
    own_out.start()

    for d in FLAT_ORDER:
        if d < 16:
            pltpu.make_async_remote_copy(
                src_ref=mine, dst_ref=place, send_sem=ag_sems.at[0],
                recv_sem=ag_sems.at[1], device_id=flat_peer(d), device_id_type=MESH,
            ).start()

    @pl.when(flat != 0)
    def _():
        pltpu.make_async_copy(shift_recv, shift_recv, shift_sems.at[0]).wait()

    @pl.when(flat == 0)
    def _():
        pieces = shift_recv.at[:, pl.ds(0, 15 * LANES)]
        pltpu.make_async_copy(pieces, pieces, shift_sems.at[0]).wait()

    pltpu.make_async_copy(piece, piece, shift_sems.at[3]).wait()

    @pl.when(flat != 15)
    def _():
        pltpu.make_async_copy(piece_low, piece_low, shift_sems.at[5]).wait()

    phi_three = phi_recv.at[:, pl.ds(0, 3)]
    pltpu.make_async_copy(phi_three, phi_three, phi_send_sem.at[0]).wait()
    pltpu.make_async_copy(e_recv, e_recv, e_sems.at[2]).wait()
    pltpu.make_async_copy(z_same, z_same, z_sems.at[2]).wait()
    pltpu.make_async_copy(z_other, z_other, z_sems.at[2]).wait()
    own_out.wait()
    ag_others = z_recv.at[pl.ds(0, 15)]
    pltpu.make_async_copy(ag_others, ag_others, ag_sems.at[0]).wait()
    pltpu.make_async_copy(ag_others, ag_others, ag_sems.at[1]).wait()


def shards(vectors, gauge_links, momentum, directions, blocks):
    nblk = vectors.shape[0]
    vec = vectors.transpose(0, 2, 3, 1, 4).reshape(nblk, 48, SITES)
    links = gauge_links.reshape(3, 18, SITES)
    return pl.pallas_call(
        kernel,
        name="elementals",
        out_shape=jax.ShapeDtypeStruct((2, 8, 1024), F32),
        in_specs=[pl.BlockSpec(memory_space=pl.ANY)] * 5,
        out_specs=pl.BlockSpec(memory_space=pl.ANY),
        scratch_shapes=[
            pltpu.SMEM((3,), jnp.int32),
            pltpu.SMEM((2,), jnp.int32),
            pltpu.SMEM((3,), jnp.int32),
            pltpu.VMEM((nblk, 48, SITES), BF16),
            pltpu.VMEM((3, 18, SITES), BF16),
            pltpu.VMEM((2, 4, 96, HALF), BF16),
            pltpu.VMEM((2, 4, 96, HALF), BF16),
            pltpu.VMEM((4, 96, HALF), F32),
            pltpu.VMEM((48, SITES), F32),
            pltpu.VMEM((48, SITES), BF16),
            pltpu.VMEM((48, SITES), BF16),
            pltpu.VMEM((48, LANES), BF16),
            pltpu.VMEM((48, LANES), BF16),
            pltpu.VMEM((8, SITES), F32),
            pltpu.VMEM((8, SITES), F32),
            pltpu.VMEM((CHUNKS, 4, 48, LANES), BF16),
            pltpu.VMEM((CHUNKS, 4, 48, LANES), BF16),
            pltpu.VMEM((CHUNKS, 1024, 6 * LANES), BF16),
            pltpu.VMEM((2, 2, 16, 8, LANES), F32),
            pltpu.VMEM((2, 31, 8, LANES), F32),
            pltpu.VMEM((2, 8, LANES), F32),
            pltpu.VMEM((16, 8, LANES), F32),
            pltpu.VMEM((8, LANES), F32),
            pltpu.SemaphoreType.DMA((5,)),
            pltpu.SemaphoreType.DMA((3,)),
            pltpu.SemaphoreType.DMA((6,)),
            pltpu.SemaphoreType.DMA((3,)),
            pltpu.SemaphoreType.DMA((1,)),
            pltpu.SemaphoreType.DMA((CHUNKS + 1,)),
            pltpu.SemaphoreType.DMA((3,)),
            pltpu.SemaphoreType.DMA((3,)),
            pltpu.SemaphoreType.DMA((2,)),
            pltpu.SemaphoreType.REGULAR((3,)),
        ],
        compiler_params=pltpu.CompilerParams(
            collective_id=1, has_side_effects=True, vmem_limit_bytes=63 * 2**20
        ),
    )(momentum, directions, blocks, vec, links)


def solution(mesh):
    in_specs = (P(None, "vec", None, "space", None), P(None, None, "space", None), P(), P(), P())
    out_specs = P(None, "vec", None)
    return jax.shard_map(shards, mesh=mesh, in_specs=in_specs, out_specs=out_specs, check_vma=False)
```

```python
import functools
import math

import jax
import jax.numpy as jnp
from jax import lax
from jax.experimental import pallas as pl
from jax.experimental.pallas import tpu as pltpu
from jax.sharding import PartitionSpec as P

LX = 32
LY = 64
SITES = LX * LY
PLANES = 128
TWO_PI = 2.0 * math.pi
MESH = pl.DeviceIdType.MESH
F32 = jnp.float32
BF16 = jnp.bfloat16
LANES = 128
QUARTER = SITES // 4
CHUNKS = QUARTER // LANES
FLAT_ORDER = sorted(range(1, 32), key=lambda d: -(min(d // 4 % 4, 4 - d // 4 % 4) + min(d % 4, 4 - d % 4)))


def link_rows(links, field):
    out = []
    for c in range(3):
        real_part = None
        for b in range(3):
            at = (c * 3 + b) * 2
            lr = links[at : at + 1]
            li = links[at + 1 : at + 2]
            fr = field[16 * b : 16 * b + 8]
            fi = field[16 * b + 8 : 16 * b + 16]
            re = lr * fr - li * fi
            im = lr * fi + li * fr
            real_part, imag_part = (re, im) if real_part is None else (real_part + re, imag_part + im)
        out += [real_part, imag_part]
    return out


def rolled(direction, row):
    lane = lax.broadcasted_iota(jnp.int32, row.shape, 1)
    next_x = pltpu.roll(row, SITES - LY, 1)
    next_y = jnp.where(
        lax.rem(lane, LY) == LY - 1, pltpu.roll(row, LY - 1, 1), pltpu.roll(row, SITES - 1, 1)
    )
    return jnp.where(direction == 0, next_x, next_y)


def kernel(
    momentum_hbm, directions_hbm, blocks_hbm, vec_hbm, links_hbm, out,
    momentum, directions, blocks, vec_v, links_v, st_send, st_recv, st_wide, roll_v, shift_send, shift_recv, piece, piece_low, cos_v, sin_v,
    phi_send, phi_recv, table, e_send, e_recv, z_send, z_recv, mine,
    load_sem, own_sem, shift_sems, st_sems, phi_send_sem, phi_recv_sems, e_sems, z_sems, ag_sems, known_sems,
):
    space = lax.axis_index("space")
    vec = lax.axis_index("vec")
    flat = lax.rem(space, 16)
    zlow = lax.div(space, 16)
    half = lax.div(vec, 2)
    core = lax.rem(vec, 2)
    zee = half * 8 + zlow

    def flat_peer(d):
        x = lax.rem(lax.div(flat, 4) + lax.rem(lax.div(d, 4), 4), 4)
        y = lax.rem(flat + lax.rem(d, 4), 4)
        return zlow * 16 + x * 4 + y, half * 2 + lax.rem(core + lax.div(d, 16), 2)

    def z_peer(d):
        z = lax.rem(zee + d, 16)
        return lax.rem(z, 8) * 16 + flat, lax.div(z, 8) * 2 + core

    def vec_peer(d):
        return space, lax.rem(vec + d, 4)

    layer = zlow * 16
    up = (lax.rem(zlow + 1, 8) * 16 + flat, vec)
    down = (lax.rem(zlow + 7, 8) * 16 + flat, vec)
    last = lax.div(flat, 15)
    near = half * 2 + (1 - core)
    cross_core = (space, (1 - half) * 2 + (1 - core))

    barrier = pltpu.get_barrier_semaphore()

    def greet(device):
        pl.semaphore_signal(barrier, inc=1, device_id=device, device_id_type=MESH)

    greet(z_peer(8))
    greet(cross_core)
    greet(z_peer(1))
    greet(z_peer(15))
    greet(up)

    @pl.loop(1, 32)
    def _(d):
        greet(flat_peer(d))

    loads = [
        pltpu.make_async_copy(source, target, load_sem.at[at])
        for at, (source, target) in enumerate(
            (
                (blocks_hbm, blocks), (directions_hbm, directions), (momentum_hbm, momentum), (links_hbm, links_v),
                *((vec_hbm.at[k], vec_v.at[k]) for k in range(vec_v.shape[0])),
            )
        )
    ]
    for load in loads:
        load.start()
    for load in loads:
        load.wait()

    def pass_on(at, steps):
        for d in (steps, 16 - steps):
            pl.semaphore_signal(known_sems.at[at], inc=1, device_id=z_peer(d), device_id_type=MESH)

    first_step = directions[0]
    z_first = first_step == 2
    inplane = jnp.where(z_first, directions[1], first_step)

    for q in range(4):
        for part in range(CHUNKS):
            at = slice(q * QUARTER + part * LANES, q * QUARTER + (part + 1) * LANES)
            st_send[part, q, 0:48] = vec_v[blocks[1], :, at]
            st_send[part, q, 48:96] = vec_v[blocks[2], :, at]

    for b in range(6):
        row = vec_v[blocks[0], (b // 2) * 16 : (b // 2) * 16 + 16, :].astype(F32)
        row = row[(b % 2) * 8 : (b % 2) * 8 + 8]
        roll_v[b * 8 : b * 8 + 8] = rolled(inplane, row)

    @pl.loop(0, SITES // 256)
    def _(t):
        at = pl.ds(t * 256, 256)
        links = links_v[inplane, :, at].astype(F32)
        moved = jnp.concatenate(link_rows(links, roll_v[:, at]), axis=0).astype(BF16)
        shift_send[:, at] = jnp.where(z_first, vec_v[blocks[0], :, at], moved)

    pl.semaphore_wait(barrier, 31 + 5)

    @pl.when(flat != 0)
    def _():
        pltpu.make_async_remote_copy(
            src_ref=shift_send, dst_ref=shift_recv, send_sem=shift_sems.at[0], recv_sem=shift_sems.at[1],
            device_id=(space - 1, vec), device_id_type=MESH,
        ).start()

    @pl.when(flat == 0)
    def _():
        pltpu.make_async_copy(shift_send.at[:, pl.ds(0, LANES)], piece, shift_sems.at[2]).start()
        for k in range(15, 0, -1):
            pltpu.make_async_remote_copy(
                src_ref=shift_send.at[:, pl.ds(k * LANES, LANES)], dst_ref=piece, send_sem=shift_sems.at[0],
                recv_sem=shift_sems.at[2], device_id=(layer + k, vec), device_id_type=MESH,
            ).start()

    def exchange(part, steps):
        for d in steps:
            target = lax.rem(vec + d, 4)
            pltpu.make_async_remote_copy(
                src_ref=st_send.at[part, target], dst_ref=st_recv.at[part, vec], send_sem=st_sems.at[CHUNKS],
                recv_sem=st_sems.at[part], device_id=vec_peer(d), device_id_type=MESH,
            ).start()

    exchange(0, (2, 1))
    exchange(1, (2, 1))
    for part in range(CHUNKS):
        pltpu.make_async_copy(st_send.at[part, vec], st_recv.at[part, vec], own_sem.at[part]).start()
    pass_on(0, 1)
    pl.semaphore_wait(known_sems.at[0], 2)
    pass_on(1, 2)
    site = lax.broadcasted_iota(jnp.int32, (8, SITES), 1)
    fraction = ((momentum[0] * lax.div(site, LY)) & (LX - 1)).astype(F32) / LX
    fraction = fraction + ((momentum[1] * lax.rem(site, LY)) & (LY - 1)).astype(F32) / LY
    fraction = fraction + ((momentum[2] * space) & (PLANES - 1)).astype(F32) / PLANES
    angles = TWO_PI * fraction
    cos_v[...] = jnp.cos(angles)
    sin_v[...] = jnp.sin(angles)

    pltpu.make_async_copy(piece, piece, shift_sems.at[2]).wait()

    def forward(dst, sem):
        pltpu.make_async_remote_copy(
            src_ref=piece, dst_ref=dst, send_sem=shift_sems.at[3], recv_sem=sem, device_id=down, device_id_type=MESH,
        ).start()

    @pl.when(flat != 15)
    def _():
        forward(piece_low, shift_sems.at[4])

    @pl.when(flat == 15)
    def _():
        forward(shift_recv.at[:, pl.ds(15 * LANES, LANES)], shift_sems.at[1])

    exchange(0, (3,))
    exchange(1, (3,))
    exchange(2, (2, 3, 1))
    exchange(3, (2, 3, 1))
    pl.semaphore_wait(known_sems.at[1], 2)
    pass_on(2, 4)

    def phase_own():
        pltpu.make_async_copy(shift_recv, shift_recv, shift_sems.at[1]).wait()

        @pl.loop(0, SITES // 256)
        def _(t):
            at = pl.ds(t * 256, 256)
            links = links_v[2, :, at].astype(F32)
            moved = jnp.concatenate(link_rows(links, shift_recv[:, at].astype(F32)), axis=0)
            shift_recv[:, at] = moved.astype(BF16)

        for b in range(6):
            row = shift_recv[(b // 2) * 16 : (b // 2) * 16 + 16, :].astype(F32)
            row = row[(b % 2) * 8 : (b % 2) * 8 + 8]
            roll_v[b * 8 : b * 8 + 8] = rolled(inplane, row)

        @pl.loop(0, SITES // LANES)
        def _(t):
            at = pl.ds(t * LANES, LANES)
            links = links_v[inplane, :, at].astype(F32)
            moved = jnp.concatenate(link_rows(links, roll_v[:, at]), axis=0).astype(BF16)
            moved = jnp.where(z_first, moved, shift_recv[:, at]).astype(F32)
            cosines = cos_v[:, at]
            sines = sin_v[:, at]
            rows = []
            for a in range(3):
                re = moved[16 * a : 16 * a + 8]
                im = moved[16 * a + 8 : 16 * a + 16]
                rows += [cosines * re + sines * im, cosines * im - sines * re]
            phi_send[lax.rem(t, CHUNKS), lax.div(t, CHUNKS)] = jnp.concatenate(rows, axis=0).astype(BF16)

        pltpu.make_async_copy(phi_send.at[:, vec], phi_recv.at[:, vec], own_sem.at[CHUNKS]).start()
        pltpu.make_async_remote_copy(
            src_ref=phi_send.at[:, near], dst_ref=phi_recv.at[:, vec], send_sem=phi_send_sem.at[0],
            recv_sem=phi_recv_sems.at[CHUNKS], device_id=(space, near), device_id_type=MESH,
        ).start()

    @pl.loop(0, 2)
    def _(turn):
        pl.when(turn == last)(phase_own)

        @pl.when((turn == 0) & (flat != 15))
        def _():
            pltpu.make_async_copy(piece_low, piece_low, shift_sems.at[4]).wait()
            pltpu.make_async_remote_copy(
                src_ref=piece_low, dst_ref=shift_recv.at[:, pl.ds(pl.multiple_of(flat * LANES, LANES), LANES)],
                send_sem=shift_sems.at[5], recv_sem=shift_sems.at[1], device_id=(layer + 15, vec), device_id_type=MESH,
            ).start()

    pl.semaphore_wait(known_sems.at[2], 2)
    def send_far():
        for n in range(CHUNKS):
            for to_vec in (cross_core[1], lax.rem(vec + 2, 4)):
                pltpu.make_async_remote_copy(
                    src_ref=phi_send.at[n, to_vec], dst_ref=phi_recv.at[n, vec], send_sem=phi_send_sem.at[0],
                    recv_sem=phi_recv_sems.at[n], device_id=(space, to_vec), device_id_type=MESH,
                ).start()

    st_three = st_recv.at[0, pl.ds(0, 3)]

    def make_table(part):
        own_st = st_recv.at[part, 0]
        pltpu.make_async_copy(own_st, own_st, own_sem.at[part]).wait()
        pltpu.make_async_copy(st_three, st_three, st_sems.at[part]).wait()

        @pl.loop(0, 4)
        def _(source):
            st_wide[source] = st_recv[part, source].astype(F32)

        @pl.loop(0, 4)
        def _(source):
            right = [[st_wide[k, 48 + 8 * b : 56 + 8 * b] for b in range(6)] for k in range(4)]
            for j in range(8):
                left = [
                    jnp.broadcast_to(st_wide[source, 8 * b + j : 8 * b + j + 1], (8, LANES)) for b in range(6)
                ]
                start = source * 256 + j * 32
                for a in range(3):
                    b = 2 * ((a + 1) % 3)
                    c = 2 * ((a + 2) % 3)
                    reals = []
                    imags = []
                    for k in range(4):
                        rbr, rbi, rcr, rci = right[k][b], right[k][b + 1], right[k][c], right[k][c + 1]
                        lbr, lbi, lcr, lci = left[b], left[b + 1], left[c], left[c + 1]
                        reals.append(lbr * rcr - lbi * rci - (lcr * rbr - lci * rbi))
                        imags.append(lbr * rci + lbi * rcr - (lcr * rbi + lci * rbr))
                    table[part, pl.ds(start, 32), 2 * a * LANES : (2 * a + 1) * LANES] = jnp.concatenate(
                        reals, axis=0
                    ).astype(BF16)
                    table[part, pl.ds(start, 32), (2 * a + 1) * LANES : (2 * a + 2) * LANES] = jnp.concatenate(
                        imags, axis=0
                    ).astype(BF16)

    def product(n, whose):
        real_rows = []
        imag_rows = []
        for c in range(2):
            field = phi_recv[n, 2 * whose + c].astype(F32)
            reals = [field[16 * a : 16 * a + 8] for a in range(3)]
            imags = [field[16 * a + 8 : 16 * a + 16] for a in range(3)]
            real_rows.append(jnp.concatenate([x for a in range(3) for x in (reals[a], -imags[a])], axis=1))
            imag_rows.append(jnp.concatenate([x for a in range(3) for x in (imags[a], reals[a])], axis=1))
        rows = jnp.concatenate(real_rows + imag_rows, axis=0).astype(BF16)
        return lax.dot_general(rows, table[n], (((1,), (1,)), ((), ())), preferred_element_type=F32)

    def scatter(at, total):
        for part in range(2):
            for c in range(2):
                start = part * 16 + c * 8
                for tile in range(8):
                    e_send[at, c, part * 8 + tile] = total[start : start + 8, tile * LANES : (tile + 1) * LANES]
        for d in FLAT_ORDER:
            to_space, to_vec = flat_peer(d)
            pltpu.make_async_remote_copy(
                src_ref=e_send.at[at, lax.rem(to_vec, 2), lax.rem(to_space, 16)], dst_ref=e_recv.at[at, d - 1],
                send_sem=e_sems.at[2], recv_sem=e_sems.at[at], device_id=(to_space, to_vec), device_id_type=MESH,
            ).start()

    def gathered(at):
        pltpu.make_async_copy(e_recv.at[at], e_recv.at[at], e_sems.at[at]).wait()
        total = e_send[at, core, flat]
        for d in range(31):
            total = total + e_recv[at, d]
        return total

    def send_z(at, d):
        to_space, to_vec = z_peer(d)
        pltpu.make_async_remote_copy(
            src_ref=z_send.at[at], dst_ref=z_recv.at[zee], send_sem=z_sems.at[2],
            recv_sem=z_sems.at[at], device_id=(to_space, to_vec), device_id_type=MESH,
        ).start()

    make_table(0)
    make_table(1)
    for part in range(CHUNKS):
        pltpu.make_async_copy(st_three, st_three, st_sems.at[CHUNKS]).wait()
    send_far()
    phi_near = phi_recv.at[:, 0]
    pltpu.make_async_copy(phi_near, phi_near, own_sem.at[CHUNKS]).wait()
    pltpu.make_async_copy(phi_near, phi_near, phi_recv_sems.at[CHUNKS]).wait()
    total = product(0, half) + product(1, half)
    for n in (2, 3):
        make_table(n)
        total = total + product(n, half)
    scatter(0, total)

    total = None
    for n in range(CHUNKS):
        phi_two = phi_recv.at[n, pl.ds(0, 2)]
        pltpu.make_async_copy(phi_two, phi_two, phi_recv_sems.at[n]).wait()
        term = product(n, 1 - half)
        total = term if total is None else total + term
    scatter(1, total)

    z_send[0] = gathered(0)
    z_recv[zee] = z_send[0]
    for step in range(1, 8):
        send_z(0, half * 8 + lax.rem(zlow + step, 8) - zee + 16)

    z_send[1] = gathered(1)
    for step in (0, 1, 7, 2, 6, 3, 5, 4):
        send_z(1, (1 - half) * 8 + lax.rem(zlow + step, 8) - zee + 16)

    @pl.when(flat != 0)
    def _():
        pltpu.make_async_copy(shift_recv, shift_recv, shift_sems.at[0]).wait()

    @pl.when(flat == 0)
    def _():
        pieces = shift_recv.at[:, pl.ds(0, 15 * LANES)]
        pltpu.make_async_copy(pieces, pieces, shift_sems.at[0]).wait()

    pltpu.make_async_copy(piece, piece, shift_sems.at[3]).wait()

    @pl.when(flat != 15)
    def _():
        pltpu.make_async_copy(piece_low, piece_low, shift_sems.at[5]).wait()

    phi_three = phi_recv.at[:, pl.ds(0, 3)]
    pltpu.make_async_copy(phi_three, phi_three, phi_send_sem.at[0]).wait()
    pltpu.make_async_copy(e_recv, e_recv, e_sems.at[2]).wait()

    z_same = z_recv.at[pl.ds(0, 7)]
    z_other = z_recv.at[pl.ds(0, 8)]
    pltpu.make_async_copy(z_same, z_same, z_sems.at[0]).wait()
    pltpu.make_async_copy(z_other, z_other, z_sems.at[1]).wait()
    whole = z_recv[0]
    for z in range(1, 16):
        whole = whole + z_recv[z]
    mine[...] = whole * (1.0 / math.sqrt(SITES * PLANES))
    place = out.at[lax.div(flat, 8), :, pl.ds(pl.multiple_of(lax.rem(flat, 8) * LANES, LANES), LANES)]
    own_out = pltpu.make_async_copy(mine, place, load_sem.at[0])
    own_out.start()

    for d in FLAT_ORDER:
        if d < 16:
            pltpu.make_async_remote_copy(
                src_ref=mine, dst_ref=place, send_sem=ag_sems.at[0],
                recv_sem=ag_sems.at[1], device_id=flat_peer(d), device_id_type=MESH,
            ).start()

    pltpu.make_async_copy(z_same, z_same, z_sems.at[2]).wait()
    pltpu.make_async_copy(z_other, z_other, z_sems.at[2]).wait()
    own_out.wait()
    ag_others = z_recv.at[pl.ds(0, 15)]
    pltpu.make_async_copy(ag_others, ag_others, ag_sems.at[0]).wait()
    pltpu.make_async_copy(ag_others, ag_others, ag_sems.at[1]).wait()


def shards(vectors, gauge_links, momentum, directions, blocks):
    nblk = vectors.shape[0]
    vec = vectors.transpose(0, 2, 3, 1, 4).reshape(nblk, 48, SITES)
    links = gauge_links.reshape(3, 18, SITES)
    return pl.pallas_call(
        kernel,
        name="elementals",
        out_shape=jax.ShapeDtypeStruct((2, 8, 1024), F32),
        in_specs=[pl.BlockSpec(memory_space=pl.ANY)] * 5,
        out_specs=pl.BlockSpec(memory_space=pl.ANY),
        scratch_shapes=[
            pltpu.SMEM((3,), jnp.int32),
            pltpu.SMEM((2,), jnp.int32),
            pltpu.SMEM((3,), jnp.int32),
            pltpu.VMEM((nblk, 48, SITES), BF16),
            pltpu.VMEM((3, 18, SITES), BF16),
            pltpu.VMEM((CHUNKS, 4, 96, LANES), BF16),
            pltpu.VMEM((CHUNKS, 4, 96, LANES), BF16),
            pltpu.VMEM((4, 96, LANES), F32),
            pltpu.VMEM((48, SITES), F32),
            pltpu.VMEM((48, SITES), BF16),
            pltpu.VMEM((48, SITES), BF16),
            pltpu.VMEM((48, LANES), BF16),
            pltpu.VMEM((48, LANES), BF16),
            pltpu.VMEM((8, SITES), F32),
            pltpu.VMEM((8, SITES), F32),
            pltpu.VMEM((CHUNKS, 4, 48, LANES), BF16),
            pltpu.VMEM((CHUNKS, 4, 48, LANES), BF16),
            pltpu.VMEM((CHUNKS, 1024, 6 * LANES), BF16),
            pltpu.VMEM((2, 2, 16, 8, LANES), F32),
            pltpu.VMEM((2, 31, 8, LANES), F32),
            pltpu.VMEM((2, 8, LANES), F32),
            pltpu.VMEM((16, 8, LANES), F32),
            pltpu.VMEM((8, LANES), F32),
            pltpu.SemaphoreType.DMA((4 + nblk,)),
            pltpu.SemaphoreType.DMA((CHUNKS + 1,)),
            pltpu.SemaphoreType.DMA((6,)),
            pltpu.SemaphoreType.DMA((CHUNKS + 1,)),
            pltpu.SemaphoreType.DMA((1,)),
            pltpu.SemaphoreType.DMA((CHUNKS + 1,)),
            pltpu.SemaphoreType.DMA((3,)),
            pltpu.SemaphoreType.DMA((3,)),
            pltpu.SemaphoreType.DMA((2,)),
            pltpu.SemaphoreType.REGULAR((3,)),
        ],
        compiler_params=pltpu.CompilerParams(
            collective_id=1, has_side_effects=True, vmem_limit_bytes=63 * 2**20
        ),
    )(momentum, directions, blocks, vec, links)


def solution(mesh):
    in_specs = (P(None, "vec", None, "space", None), P(None, None, "space", None), P(), P(), P())
    out_specs = P(None, "vec", None)
    return jax.shard_map(shards, mesh=mesh, in_specs=in_specs, out_specs=out_specs, check_vma=False)
```

```python
import functools
import math

import jax
import jax.numpy as jnp
from jax import lax
from jax.experimental import pallas as pl
from jax.experimental.pallas import tpu as pltpu
from jax.sharding import PartitionSpec as P

LX = 32
LY = 64
SITES = LX * LY
PLANES = 128
TWO_PI = 2.0 * math.pi
MESH = pl.DeviceIdType.MESH
F32 = jnp.float32
BF16 = jnp.bfloat16
LANES = 128
QUARTER = SITES // 4
CHUNKS = QUARTER // LANES
FLAT_ORDER = sorted(range(1, 32), key=lambda d: -(min(d // 4 % 4, 4 - d // 4 % 4) + min(d % 4, 4 - d % 4)))


def link_rows(links, field):
    out = []
    for c in range(3):
        real_part = None
        for b in range(3):
            at = (c * 3 + b) * 2
            lr = links[at : at + 1]
            li = links[at + 1 : at + 2]
            fr = field[16 * b : 16 * b + 8]
            fi = field[16 * b + 8 : 16 * b + 16]
            re = lr * fr - li * fi
            im = lr * fi + li * fr
            real_part, imag_part = (re, im) if real_part is None else (real_part + re, imag_part + im)
        out += [real_part, imag_part]
    return out


def rolled(direction, row):
    lane = lax.broadcasted_iota(jnp.int32, row.shape, 1)
    next_x = pltpu.roll(row, SITES - LY, 1)
    next_y = jnp.where(
        lax.rem(lane, LY) == LY - 1, pltpu.roll(row, LY - 1, 1), pltpu.roll(row, SITES - 1, 1)
    )
    return jnp.where(direction == 0, next_x, next_y)


def kernel(
    momentum_hbm, directions_hbm, blocks_hbm, vec_hbm, links_hbm, out,
    momentum, directions, blocks, vec_v, links_v, st_send, st_recv, st_wide, roll_v, shift_send, shift_recv, piece, piece_low, cos_v, sin_v,
    phi_send, phi_recv, table, e_send, e_recv, z_send, z_recv, mine,
    load_sem, own_sem, shift_sems, st_sems, phi_send_sem, phi_recv_sems, e_sems, z_sems, ag_sems, known_sems,
):
    space = lax.axis_index("space")
    vec = lax.axis_index("vec")
    flat = lax.rem(space, 16)
    zlow = lax.div(space, 16)
    half = lax.div(vec, 2)
    core = lax.rem(vec, 2)
    zee = half * 8 + zlow

    def flat_peer(d):
        x = lax.rem(lax.div(flat, 4) + lax.rem(lax.div(d, 4), 4), 4)
        y = lax.rem(flat + lax.rem(d, 4), 4)
        return zlow * 16 + x * 4 + y, half * 2 + lax.rem(core + lax.div(d, 16), 2)

    def z_peer(d):
        z = lax.rem(zee + d, 16)
        return lax.rem(z, 8) * 16 + flat, lax.div(z, 8) * 2 + core

    def vec_peer(d):
        return space, lax.rem(vec + d, 4)

    layer = zlow * 16
    up = (lax.rem(zlow + 1, 8) * 16 + flat, vec)
    down = (lax.rem(zlow + 7, 8) * 16 + flat, vec)
    last = lax.div(flat, 15)
    near = half * 2 + (1 - core)
    cross_core = (space, (1 - half) * 2 + (1 - core))

    barrier = pltpu.get_barrier_semaphore()

    def greet(device):
        pl.semaphore_signal(barrier, inc=1, device_id=device, device_id_type=MESH)

    greet(z_peer(8))
    greet(cross_core)
    greet(z_peer(1))
    greet(z_peer(15))
    greet(up)

    @pl.loop(1, 32)
    def _(d):
        greet(flat_peer(d))

    loads = [
        pltpu.make_async_copy(source, target, load_sem.at[at])
        for at, (source, target) in enumerate(
            (
                (blocks_hbm, blocks), (directions_hbm, directions), (momentum_hbm, momentum), (links_hbm, links_v),
                *((vec_hbm.at[k], vec_v.at[k]) for k in range(vec_v.shape[0])),
            )
        )
    ]
    for load in loads:
        load.start()
    for load in loads:
        load.wait()

    def pass_on(at, steps):
        for d in (steps, 16 - steps):
            pl.semaphore_signal(known_sems.at[at], inc=1, device_id=z_peer(d), device_id_type=MESH)

    first_step = directions[0]
    z_first = first_step == 2
    inplane = jnp.where(z_first, directions[1], first_step)

    for q in range(4):
        for part in range(CHUNKS):
            at = slice(q * QUARTER + part * LANES, q * QUARTER + (part + 1) * LANES)
            st_send[part, q, 0:48] = vec_v[blocks[1], :, at]
            st_send[part, q, 48:96] = vec_v[blocks[2], :, at]

    for b in range(6):
        row = vec_v[blocks[0], (b // 2) * 16 : (b // 2) * 16 + 16, :].astype(F32)
        row = row[(b % 2) * 8 : (b % 2) * 8 + 8]
        roll_v[b * 8 : b * 8 + 8] = rolled(inplane, row)

    @pl.loop(0, SITES // 256)
    def _(t):
        at = pl.ds(t * 256, 256)
        links = links_v[inplane, :, at].astype(F32)
        moved = jnp.concatenate(link_rows(links, roll_v[:, at]), axis=0).astype(BF16)
        shift_send[:, at] = jnp.where(z_first, vec_v[blocks[0], :, at], moved)

    pl.semaphore_wait(barrier, 31 + 5)

    @pl.when(flat != 0)
    def _():
        pltpu.make_async_remote_copy(
            src_ref=shift_send, dst_ref=shift_recv, send_sem=shift_sems.at[0], recv_sem=shift_sems.at[1],
            device_id=(space - 1, vec), device_id_type=MESH,
        ).start()

    @pl.when(flat == 0)
    def _():
        pltpu.make_async_copy(shift_send.at[:, pl.ds(0, LANES)], piece, shift_sems.at[2]).start()
        for k in range(15, 0, -1):
            pltpu.make_async_remote_copy(
                src_ref=shift_send.at[:, pl.ds(k * LANES, LANES)], dst_ref=piece, send_sem=shift_sems.at[0],
                recv_sem=shift_sems.at[2], device_id=(layer + k, vec), device_id_type=MESH,
            ).start()

    def exchange(part, steps):
        for d in steps:
            target = lax.rem(vec + d, 4)
            pltpu.make_async_remote_copy(
                src_ref=st_send.at[part, target], dst_ref=st_recv.at[part, vec], send_sem=st_sems.at[CHUNKS],
                recv_sem=st_sems.at[part], device_id=vec_peer(d), device_id_type=MESH,
            ).start()

    exchange(0, (2, 1))
    exchange(1, (2, 1))
    for part in range(CHUNKS):
        pltpu.make_async_copy(st_send.at[part, vec], st_recv.at[part, vec], own_sem.at[part]).start()
    pass_on(0, 1)
    pl.semaphore_wait(known_sems.at[0], 2)
    pass_on(1, 2)
    site = lax.broadcasted_iota(jnp.int32, (8, SITES), 1)
    fraction = ((momentum[0] * lax.div(site, LY)) & (LX - 1)).astype(F32) / LX
    fraction = fraction + ((momentum[1] * lax.rem(site, LY)) & (LY - 1)).astype(F32) / LY
    fraction = fraction + ((momentum[2] * space) & (PLANES - 1)).astype(F32) / PLANES
    angles = TWO_PI * fraction
    cos_v[...] = jnp.cos(angles)
    sin_v[...] = jnp.sin(angles)

    pltpu.make_async_copy(piece, piece, shift_sems.at[2]).wait()

    def forward(dst, sem):
        pltpu.make_async_remote_copy(
            src_ref=piece, dst_ref=dst, send_sem=shift_sems.at[3], recv_sem=sem, device_id=down, device_id_type=MESH,
        ).start()

    @pl.when(flat != 15)
    def _():
        forward(piece_low, shift_sems.at[4])

    @pl.when(flat == 15)
    def _():
        forward(shift_recv.at[:, pl.ds(15 * LANES, LANES)], shift_sems.at[1])

    exchange(0, (3,))
    exchange(1, (3,))
    exchange(2, (2, 3, 1))
    exchange(3, (2, 3, 1))
    pl.semaphore_wait(known_sems.at[1], 2)
    pass_on(2, 4)

    def phase_own():
        pltpu.make_async_copy(shift_recv, shift_recv, shift_sems.at[1]).wait()

        @pl.loop(0, SITES // 256)
        def _(t):
            at = pl.ds(t * 256, 256)
            links = links_v[2, :, at].astype(F32)
            moved = jnp.concatenate(link_rows(links, shift_recv[:, at].astype(F32)), axis=0)
            shift_recv[:, at] = moved.astype(BF16)

        for b in range(6):
            row = shift_recv[(b // 2) * 16 : (b // 2) * 16 + 16, :].astype(F32)
            row = row[(b % 2) * 8 : (b % 2) * 8 + 8]
            roll_v[b * 8 : b * 8 + 8] = rolled(inplane, row)

        @pl.loop(0, SITES // LANES)
        def _(t):
            at = pl.ds(t * LANES, LANES)
            links = links_v[inplane, :, at].astype(F32)
            moved = jnp.concatenate(link_rows(links, roll_v[:, at]), axis=0).astype(BF16)
            moved = jnp.where(z_first, moved, shift_recv[:, at]).astype(F32)
            cosines = cos_v[:, at]
            sines = sin_v[:, at]
            rows = []
            for a in range(3):
                re = moved[16 * a : 16 * a + 8]
                im = moved[16 * a + 8 : 16 * a + 16]
                rows += [cosines * re + sines * im, cosines * im - sines * re]
            phi_send[lax.rem(t, CHUNKS), lax.div(t, CHUNKS)] = jnp.concatenate(rows, axis=0).astype(BF16)

        pltpu.make_async_copy(phi_send.at[:, vec], phi_recv.at[:, vec], own_sem.at[CHUNKS]).start()
        pltpu.make_async_remote_copy(
            src_ref=phi_send.at[:, near], dst_ref=phi_recv.at[:, vec], send_sem=phi_send_sem.at[0],
            recv_sem=phi_recv_sems.at[CHUNKS], device_id=(space, near), device_id_type=MESH,
        ).start()

    @pl.loop(0, 2)
    def _(turn):
        pl.when(turn == last)(phase_own)

        @pl.when((turn == 0) & (flat != 15))
        def _():
            pltpu.make_async_copy(piece_low, piece_low, shift_sems.at[4]).wait()
            pltpu.make_async_remote_copy(
                src_ref=piece_low, dst_ref=shift_recv.at[:, pl.ds(pl.multiple_of(flat * LANES, LANES), LANES)],
                send_sem=shift_sems.at[5], recv_sem=shift_sems.at[1], device_id=(layer + 15, vec), device_id_type=MESH,
            ).start()

    pl.semaphore_wait(known_sems.at[2], 2)
    def send_far():
        for n in range(CHUNKS):
            for to_vec in (cross_core[1], lax.rem(vec + 2, 4)):
                pltpu.make_async_remote_copy(
                    src_ref=phi_send.at[n, to_vec], dst_ref=phi_recv.at[n, vec], send_sem=phi_send_sem.at[0],
                    recv_sem=phi_recv_sems.at[n], device_id=(space, to_vec), device_id_type=MESH,
                ).start()

    st_three = st_recv.at[0, pl.ds(0, 3)]

    def make_table(part):
        own_st = st_recv.at[part, 0]
        pltpu.make_async_copy(own_st, own_st, own_sem.at[part]).wait()
        pltpu.make_async_copy(st_three, st_three, st_sems.at[part]).wait()

        @pl.loop(0, 4)
        def _(source):
            st_wide[source] = st_recv[part, source].astype(F32)

        @pl.loop(0, 4)
        def _(source):
            right = [[st_wide[k, 48 + 8 * b : 56 + 8 * b] for b in range(6)] for k in range(4)]
            for j in range(8):
                left = [
                    jnp.broadcast_to(st_wide[source, 8 * b + j : 8 * b + j + 1], (8, LANES)) for b in range(6)
                ]
                start = source * 256 + j * 32
                for a in range(3):
                    b = 2 * ((a + 1) % 3)
                    c = 2 * ((a + 2) % 3)
                    reals = []
                    imags = []
                    for k in range(4):
                        rbr, rbi, rcr, rci = right[k][b], right[k][b + 1], right[k][c], right[k][c + 1]
                        lbr, lbi, lcr, lci = left[b], left[b + 1], left[c], left[c + 1]
                        reals.append(lbr * rcr - lbi * rci - (lcr * rbr - lci * rbi))
                        imags.append(lbr * rci + lbi * rcr - (lcr * rbi + lci * rbr))
                    table[part, pl.ds(start, 32), 2 * a * LANES : (2 * a + 1) * LANES] = jnp.concatenate(
                        reals, axis=0
                    ).astype(BF16)
                    table[part, pl.ds(start, 32), (2 * a + 1) * LANES : (2 * a + 2) * LANES] = jnp.concatenate(
                        imags, axis=0
                    ).astype(BF16)

    def product(n, whose):
        real_rows = []
        imag_rows = []
        for c in range(2):
            field = phi_recv[n, 2 * whose + c].astype(F32)
            reals = [field[16 * a : 16 * a + 8] for a in range(3)]
            imags = [field[16 * a + 8 : 16 * a + 16] for a in range(3)]
            real_rows.append(jnp.concatenate([x for a in range(3) for x in (reals[a], -imags[a])], axis=1))
            imag_rows.append(jnp.concatenate([x for a in range(3) for x in (imags[a], reals[a])], axis=1))
        rows = jnp.concatenate(real_rows + imag_rows, axis=0).astype(BF16)
        return lax.dot_general(rows, table[n], (((1,), (1,)), ((), ())), preferred_element_type=F32)

    def scatter(at, total):
        for part in range(2):
            for c in range(2):
                start = part * 16 + c * 8
                for tile in range(8):
                    e_send[at, c, part * 8 + tile] = total[start : start + 8, tile * LANES : (tile + 1) * LANES]
        for d in FLAT_ORDER:
            to_space, to_vec = flat_peer(d)
            pltpu.make_async_remote_copy(
                src_ref=e_send.at[at, lax.rem(to_vec, 2), lax.rem(to_space, 16)], dst_ref=e_recv.at[at, d - 1],
                send_sem=e_sems.at[2], recv_sem=e_sems.at[at], device_id=(to_space, to_vec), device_id_type=MESH,
            ).start()

    def gathered(at):
        pltpu.make_async_copy(e_recv.at[at], e_recv.at[at], e_sems.at[at]).wait()
        total = e_send[at, core, flat]
        for d in range(31):
            total = total + e_recv[at, d]
        return total

    def send_z(at, d):
        to_space, to_vec = z_peer(d)
        pltpu.make_async_remote_copy(
            src_ref=z_send.at[at], dst_ref=z_recv.at[zee], send_sem=z_sems.at[2],
            recv_sem=z_sems.at[at], device_id=(to_space, to_vec), device_id_type=MESH,
        ).start()

    def send_late():
        for part in range(CHUNKS):
            pltpu.make_async_copy(st_three, st_three, st_sems.at[CHUNKS]).wait()
        send_far()

    pl.when(flat == 15)(send_late)
    make_table(0)
    make_table(1)
    pl.when(flat != 15)(send_late)
    phi_near = phi_recv.at[:, 0]
    pltpu.make_async_copy(phi_near, phi_near, own_sem.at[CHUNKS]).wait()
    pltpu.make_async_copy(phi_near, phi_near, phi_recv_sems.at[CHUNKS]).wait()
    total = product(0, half) + product(1, half)
    for n in (2, 3):
        make_table(n)
        total = total + product(n, half)
    scatter(0, total)

    total = None
    for n in range(CHUNKS):
        phi_two = phi_recv.at[n, pl.ds(0, 2)]
        pltpu.make_async_copy(phi_two, phi_two, phi_recv_sems.at[n]).wait()
        term = product(n, 1 - half)
        total = term if total is None else total + term
    scatter(1, total)

    z_send[0] = gathered(0)
    z_recv[zee] = z_send[0]
    for step in range(1, 8):
        send_z(0, half * 8 + lax.rem(zlow + step, 8) - zee + 16)

    z_send[1] = gathered(1)
    for step in (0, 1, 7, 2, 6, 3, 5, 4):
        send_z(1, (1 - half) * 8 + lax.rem(zlow + step, 8) - zee + 16)

    @pl.when(flat != 0)
    def _():
        pltpu.make_async_copy(shift_recv, shift_recv, shift_sems.at[0]).wait()

    @pl.when(flat == 0)
    def _():
        pieces = shift_recv.at[:, pl.ds(0, 15 * LANES)]
        pltpu.make_async_copy(pieces, pieces, shift_sems.at[0]).wait()

    pltpu.make_async_copy(piece, piece, shift_sems.at[3]).wait()

    @pl.when(flat != 15)
    def _():
        pltpu.make_async_copy(piece_low, piece_low, shift_sems.at[5]).wait()

    phi_three = phi_recv.at[:, pl.ds(0, 3)]
    pltpu.make_async_copy(phi_three, phi_three, phi_send_sem.at[0]).wait()
    pltpu.make_async_copy(e_recv, e_recv, e_sems.at[2]).wait()

    z_same = z_recv.at[pl.ds(0, 7)]
    z_other = z_recv.at[pl.ds(0, 8)]
    pltpu.make_async_copy(z_same, z_same, z_sems.at[0]).wait()
    pltpu.make_async_copy(z_other, z_other, z_sems.at[1]).wait()
    whole = z_recv[0]
    for z in range(1, 16):
        whole = whole + z_recv[z]
    mine[...] = whole * (1.0 / math.sqrt(SITES * PLANES))
    place = out.at[lax.div(flat, 8), :, pl.ds(pl.multiple_of(lax.rem(flat, 8) * LANES, LANES), LANES)]
    own_out = pltpu.make_async_copy(mine, place, load_sem.at[0])
    own_out.start()

    for d in FLAT_ORDER:
        if d < 16:
            pltpu.make_async_remote_copy(
                src_ref=mine, dst_ref=place, send_sem=ag_sems.at[0],
                recv_sem=ag_sems.at[1], device_id=flat_peer(d), device_id_type=MESH,
            ).start()

    pltpu.make_async_copy(z_same, z_same, z_sems.at[2]).wait()
    pltpu.make_async_copy(z_other, z_other, z_sems.at[2]).wait()
    own_out.wait()
    ag_others = z_recv.at[pl.ds(0, 15)]
    pltpu.make_async_copy(ag_others, ag_others, ag_sems.at[0]).wait()
    pltpu.make_async_copy(ag_others, ag_others, ag_sems.at[1]).wait()


def shards(vectors, gauge_links, momentum, directions, blocks):
    nblk = vectors.shape[0]
    vec = vectors.transpose(0, 2, 3, 1, 4).reshape(nblk, 48, SITES)
    links = gauge_links.reshape(3, 18, SITES)
    return pl.pallas_call(
        kernel,
        name="elementals",
        out_shape=jax.ShapeDtypeStruct((2, 8, 1024), F32),
        in_specs=[pl.BlockSpec(memory_space=pl.ANY)] * 5,
        out_specs=pl.BlockSpec(memory_space=pl.ANY),
        scratch_shapes=[
            pltpu.SMEM((3,), jnp.int32),
            pltpu.SMEM((2,), jnp.int32),
            pltpu.SMEM((3,), jnp.int32),
            pltpu.VMEM((nblk, 48, SITES), BF16),
            pltpu.VMEM((3, 18, SITES), BF16),
            pltpu.VMEM((CHUNKS, 4, 96, LANES), BF16),
            pltpu.VMEM((CHUNKS, 4, 96, LANES), BF16),
            pltpu.VMEM((4, 96, LANES), F32),
            pltpu.VMEM((48, SITES), F32),
            pltpu.VMEM((48, SITES), BF16),
            pltpu.VMEM((48, SITES), BF16),
            pltpu.VMEM((48, LANES), BF16),
            pltpu.VMEM((48, LANES), BF16),
            pltpu.VMEM((8, SITES), F32),
            pltpu.VMEM((8, SITES), F32),
            pltpu.VMEM((CHUNKS, 4, 48, LANES), BF16),
            pltpu.VMEM((CHUNKS, 4, 48, LANES), BF16),
            pltpu.VMEM((CHUNKS, 1024, 6 * LANES), BF16),
            pltpu.VMEM((2, 2, 16, 8, LANES), F32),
            pltpu.VMEM((2, 31, 8, LANES), F32),
            pltpu.VMEM((2, 8, LANES), F32),
            pltpu.VMEM((16, 8, LANES), F32),
            pltpu.VMEM((8, LANES), F32),
            pltpu.SemaphoreType.DMA((4 + nblk,)),
            pltpu.SemaphoreType.DMA((CHUNKS + 1,)),
            pltpu.SemaphoreType.DMA((6,)),
            pltpu.SemaphoreType.DMA((CHUNKS + 1,)),
            pltpu.SemaphoreType.DMA((1,)),
            pltpu.SemaphoreType.DMA((CHUNKS + 1,)),
            pltpu.SemaphoreType.DMA((3,)),
            pltpu.SemaphoreType.DMA((3,)),
            pltpu.SemaphoreType.DMA((2,)),
            pltpu.SemaphoreType.REGULAR((3,)),
        ],
        compiler_params=pltpu.CompilerParams(
            collective_id=1, has_side_effects=True, vmem_limit_bytes=63 * 2**20
        ),
    )(momentum, directions, blocks, vec, links)


def solution(mesh):
    in_specs = (P(None, "vec", None, "space", None), P(None, None, "space", None), P(), P(), P())
    out_specs = P(None, "vec", None)
    return jax.shard_map(shards, mesh=mesh, in_specs=in_specs, out_specs=out_specs, check_vma=False)
```

```python
import functools
import math

import jax
import jax.numpy as jnp
from jax import lax
from jax.experimental import pallas as pl
from jax.experimental.pallas import tpu as pltpu
from jax.sharding import PartitionSpec as P

LX = 32
LY = 64
SITES = LX * LY
PLANES = 128
TWO_PI = 2.0 * math.pi
MESH = pl.DeviceIdType.MESH
F32 = jnp.float32
BF16 = jnp.bfloat16
LANES = 128
QUARTER = SITES // 4
CHUNKS = QUARTER // LANES
FLAT_ORDER = sorted(range(1, 32), key=lambda d: -(min(d // 4 % 4, 4 - d // 4 % 4) + min(d % 4, 4 - d % 4)))


def link_rows(links, field):
    out = []
    for c in range(3):
        real_part = None
        for b in range(3):
            at = (c * 3 + b) * 2
            lr = links[at : at + 1]
            li = links[at + 1 : at + 2]
            fr = field[16 * b : 16 * b + 8]
            fi = field[16 * b + 8 : 16 * b + 16]
            re = lr * fr - li * fi
            im = lr * fi + li * fr
            real_part, imag_part = (re, im) if real_part is None else (real_part + re, imag_part + im)
        out += [real_part, imag_part]
    return out


def rolled(direction, row):
    lane = lax.broadcasted_iota(jnp.int32, row.shape, 1)
    next_x = pltpu.roll(row, SITES - LY, 1)
    next_y = jnp.where(
        lax.rem(lane, LY) == LY - 1, pltpu.roll(row, LY - 1, 1), pltpu.roll(row, SITES - 1, 1)
    )
    return jnp.where(direction == 0, next_x, next_y)


def kernel(
    momentum_hbm, directions_hbm, blocks_hbm, vec_hbm, links_hbm, out,
    momentum, directions, blocks, vec_v, links_v, st_send, st_recv, st_wide, roll_v, shift_send, shift_recv, piece, piece_low, cos_v, sin_v,
    phi_send, phi_recv, table, e_send, e_recv, z_send, z_recv, mine,
    load_sem, own_sem, shift_sems, st_sems, phi_send_sem, phi_recv_sems, e_sems, z_sems, ag_sems, known_sems,
):
    space = lax.axis_index("space")
    vec = lax.axis_index("vec")
    flat = lax.rem(space, 16)
    zlow = lax.div(space, 16)
    half = lax.div(vec, 2)
    core = lax.rem(vec, 2)
    zee = half * 8 + zlow

    def flat_peer(d):
        x = lax.rem(lax.div(flat, 4) + lax.rem(lax.div(d, 4), 4), 4)
        y = lax.rem(flat + lax.rem(d, 4), 4)
        return zlow * 16 + x * 4 + y, half * 2 + lax.rem(core + lax.div(d, 16), 2)

    def z_peer(d):
        z = lax.rem(zee + d, 16)
        return lax.rem(z, 8) * 16 + flat, lax.div(z, 8) * 2 + core

    def vec_peer(d):
        return space, lax.rem(vec + d, 4)

    layer = zlow * 16
    up = (lax.rem(zlow + 1, 8) * 16 + flat, vec)
    down = (lax.rem(zlow + 7, 8) * 16 + flat, vec)
    last = lax.div(flat, 15)
    near = half * 2 + (1 - core)
    cross_core = (space, (1 - half) * 2 + (1 - core))

    barrier = pltpu.get_barrier_semaphore()

    def greet(device):
        pl.semaphore_signal(barrier, inc=1, device_id=device, device_id_type=MESH)

    greet(z_peer(8))
    greet(cross_core)
    greet(z_peer(1))
    greet(z_peer(15))
    greet(up)

    @pl.loop(1, 32)
    def _(d):
        greet(flat_peer(d))

    loads = [
        pltpu.make_async_copy(source, target, load_sem.at[at])
        for at, (source, target) in enumerate(
            (
                (blocks_hbm, blocks), (directions_hbm, directions), (momentum_hbm, momentum), (links_hbm, links_v),
                *((vec_hbm.at[k], vec_v.at[k]) for k in range(vec_v.shape[0])),
            )
        )
    ]
    for load in loads:
        load.start()
    for load in loads:
        load.wait()

    def pass_on(at, steps):
        for d in (steps, 16 - steps):
            pl.semaphore_signal(known_sems.at[at], inc=1, device_id=z_peer(d), device_id_type=MESH)

    first_step = directions[0]
    z_first = first_step == 2
    inplane = jnp.where(z_first, directions[1], first_step)

    for q in range(4):
        for part in range(CHUNKS):
            at = slice(q * QUARTER + part * LANES, q * QUARTER + (part + 1) * LANES)
            st_send[part, q, 0:48] = vec_v[blocks[1], :, at]
            st_send[part, q, 48:96] = vec_v[blocks[2], :, at]

    for b in range(6):
        row = vec_v[blocks[0], (b // 2) * 16 : (b // 2) * 16 + 16, :].astype(F32)
        row = row[(b % 2) * 8 : (b % 2) * 8 + 8]
        roll_v[b * 8 : b * 8 + 8] = rolled(inplane, row)

    @pl.loop(0, SITES // 256)
    def _(t):
        at = pl.ds(t * 256, 256)
        links = links_v[inplane, :, at].astype(F32)
        moved = jnp.concatenate(link_rows(links, roll_v[:, at]), axis=0).astype(BF16)
        shift_send[:, at] = jnp.where(z_first, vec_v[blocks[0], :, at], moved)

    pl.semaphore_wait(barrier, 31 + 5)

    @pl.when(flat != 0)
    def _():
        pltpu.make_async_remote_copy(
            src_ref=shift_send, dst_ref=shift_recv, send_sem=shift_sems.at[0], recv_sem=shift_sems.at[1],
            device_id=(space - 1, vec), device_id_type=MESH,
        ).start()

    @pl.when(flat == 0)
    def _():
        pltpu.make_async_copy(shift_send.at[:, pl.ds(0, LANES)], piece, shift_sems.at[2]).start()
        for k in range(15, 0, -1):
            pltpu.make_async_remote_copy(
                src_ref=shift_send.at[:, pl.ds(k * LANES, LANES)], dst_ref=piece, send_sem=shift_sems.at[0],
                recv_sem=shift_sems.at[2], device_id=(layer + k, vec), device_id_type=MESH,
            ).start()

    def exchange(part, steps):
        for d in steps:
            target = lax.rem(vec + d, 4)
            pltpu.make_async_remote_copy(
                src_ref=st_send.at[part, target], dst_ref=st_recv.at[part, vec], send_sem=st_sems.at[CHUNKS],
                recv_sem=st_sems.at[part], device_id=vec_peer(d), device_id_type=MESH,
            ).start()

    exchange(0, (2, 1))
    exchange(1, (2, 1))
    for part in range(CHUNKS):
        pltpu.make_async_copy(st_send.at[part, vec], st_recv.at[part, vec], own_sem.at[part]).start()
    pass_on(0, 1)
    pl.semaphore_wait(known_sems.at[0], 2)
    pass_on(1, 2)
    site = lax.broadcasted_iota(jnp.int32, (8, SITES), 1)
    fraction = ((momentum[0] * lax.div(site, LY)) & (LX - 1)).astype(F32) / LX
    fraction = fraction + ((momentum[1] * lax.rem(site, LY)) & (LY - 1)).astype(F32) / LY
    fraction = fraction + ((momentum[2] * space) & (PLANES - 1)).astype(F32) / PLANES
    angles = TWO_PI * fraction
    cos_v[...] = jnp.cos(angles)
    sin_v[...] = jnp.sin(angles)

    pltpu.make_async_copy(piece, piece, shift_sems.at[2]).wait()

    def forward(dst, sem):
        pltpu.make_async_remote_copy(
            src_ref=piece, dst_ref=dst, send_sem=shift_sems.at[3], recv_sem=sem, device_id=down, device_id_type=MESH,
        ).start()

    @pl.when(flat != 15)
    def _():
        forward(piece_low, shift_sems.at[4])

    @pl.when(flat == 15)
    def _():
        forward(shift_recv.at[:, pl.ds(15 * LANES, LANES)], shift_sems.at[1])

    exchange(0, (3,))
    exchange(1, (3,))
    exchange(2, (2, 3, 1))
    exchange(3, (2, 3, 1))
    pl.semaphore_wait(known_sems.at[1], 2)
    pass_on(2, 4)

    def phase_own():
        pltpu.make_async_copy(shift_recv, shift_recv, shift_sems.at[1]).wait()

        @pl.loop(0, SITES // 256)
        def _(t):
            at = pl.ds(t * 256, 256)
            links = links_v[2, :, at].astype(F32)
            moved = jnp.concatenate(link_rows(links, shift_recv[:, at].astype(F32)), axis=0)
            shift_recv[:, at] = moved.astype(BF16)

        for b in range(6):
            row = shift_recv[(b // 2) * 16 : (b // 2) * 16 + 16, :].astype(F32)
            row = row[(b % 2) * 8 : (b % 2) * 8 + 8]
            roll_v[b * 8 : b * 8 + 8] = rolled(inplane, row)

        @pl.loop(0, SITES // LANES)
        def _(t):
            at = pl.ds(t * LANES, LANES)
            links = links_v[inplane, :, at].astype(F32)
            moved = jnp.concatenate(link_rows(links, roll_v[:, at]), axis=0).astype(BF16)
            moved = jnp.where(z_first, moved, shift_recv[:, at]).astype(F32)
            cosines = cos_v[:, at]
            sines = sin_v[:, at]
            rows = []
            for a in range(3):
                re = moved[16 * a : 16 * a + 8]
                im = moved[16 * a + 8 : 16 * a + 16]
                rows += [cosines * re + sines * im, cosines * im - sines * re]
            phi_send[lax.rem(t, CHUNKS), lax.div(t, CHUNKS)] = jnp.concatenate(rows, axis=0).astype(BF16)

        pltpu.make_async_copy(phi_send.at[:, vec], phi_recv.at[:, vec], own_sem.at[CHUNKS]).start()
        pltpu.make_async_remote_copy(
            src_ref=phi_send.at[:, near], dst_ref=phi_recv.at[:, vec], send_sem=phi_send_sem.at[0],
            recv_sem=phi_recv_sems.at[CHUNKS], device_id=(space, near), device_id_type=MESH,
        ).start()

    @pl.loop(0, 2)
    def _(turn):
        pl.when(turn == last)(phase_own)

        @pl.when((turn == 0) & (flat != 15))
        def _():
            pltpu.make_async_copy(piece_low, piece_low, shift_sems.at[4]).wait()
            pltpu.make_async_remote_copy(
                src_ref=piece_low, dst_ref=shift_recv.at[:, pl.ds(pl.multiple_of(flat * LANES, LANES), LANES)],
                send_sem=shift_sems.at[5], recv_sem=shift_sems.at[1], device_id=(layer + 15, vec), device_id_type=MESH,
            ).start()

    pl.semaphore_wait(known_sems.at[2], 2)
    def send_far():
        for n in range(CHUNKS):
            for to_vec in (cross_core[1], lax.rem(vec + 2, 4)):
                pltpu.make_async_remote_copy(
                    src_ref=phi_send.at[n, to_vec], dst_ref=phi_recv.at[n, vec], send_sem=phi_send_sem.at[0],
                    recv_sem=phi_recv_sems.at[n], device_id=(space, to_vec), device_id_type=MESH,
                ).start()

    st_three = st_recv.at[0, pl.ds(0, 3)]

    def make_table(part):
        own_st = st_recv.at[part, 0]
        pltpu.make_async_copy(own_st, own_st, own_sem.at[part]).wait()
        pltpu.make_async_copy(st_three, st_three, st_sems.at[part]).wait()

        @pl.loop(0, 4)
        def _(source):
            st_wide[source] = st_recv[part, source].astype(F32)

        @pl.loop(0, 4)
        def _(source):
            right = [[st_wide[k, 48 + 8 * b : 56 + 8 * b] for b in range(6)] for k in range(4)]
            for j in range(8):
                left = [
                    jnp.broadcast_to(st_wide[source, 8 * b + j : 8 * b + j + 1], (8, LANES)) for b in range(6)
                ]
                start = source * 256 + j * 32
                for a in range(3):
                    b = 2 * ((a + 1) % 3)
                    c = 2 * ((a + 2) % 3)
                    reals = []
                    imags = []
                    for k in range(4):
                        rbr, rbi, rcr, rci = right[k][b], right[k][b + 1], right[k][c], right[k][c + 1]
                        lbr, lbi, lcr, lci = left[b], left[b + 1], left[c], left[c + 1]
                        reals.append(lbr * rcr - lbi * rci - (lcr * rbr - lci * rbi))
                        imags.append(lbr * rci + lbi * rcr - (lcr * rbi + lci * rbr))
                    table[part, pl.ds(start, 32), 2 * a * LANES : (2 * a + 1) * LANES] = jnp.concatenate(
                        reals, axis=0
                    ).astype(BF16)
                    table[part, pl.ds(start, 32), (2 * a + 1) * LANES : (2 * a + 2) * LANES] = jnp.concatenate(
                        imags, axis=0
                    ).astype(BF16)

    def product(n, whose):
        real_rows = []
        imag_rows = []
        for c in range(2):
            field = phi_recv[n, 2 * whose + c].astype(F32)
            reals = [field[16 * a : 16 * a + 8] for a in range(3)]
            imags = [field[16 * a + 8 : 16 * a + 16] for a in range(3)]
            real_rows.append(jnp.concatenate([x for a in range(3) for x in (reals[a], -imags[a])], axis=1))
            imag_rows.append(jnp.concatenate([x for a in range(3) for x in (imags[a], reals[a])], axis=1))
        rows = jnp.concatenate(real_rows + imag_rows, axis=0).astype(BF16)
        return lax.dot_general(rows, table[n], (((1,), (1,)), ((), ())), preferred_element_type=F32)

    def scatter(at, total):
        for part in range(2):
            for c in range(2):
                start = part * 16 + c * 8
                for tile in range(8):
                    e_send[at, c, part * 8 + tile] = total[start : start + 8, tile * LANES : (tile + 1) * LANES]
        for d in FLAT_ORDER:
            to_space, to_vec = flat_peer(d)
            pltpu.make_async_remote_copy(
                src_ref=e_send.at[at, lax.rem(to_vec, 2), lax.rem(to_space, 16)], dst_ref=e_recv.at[at, d - 1],
                send_sem=e_sems.at[2], recv_sem=e_sems.at[at], device_id=(to_space, to_vec), device_id_type=MESH,
            ).start()

    def gathered(at):
        pltpu.make_async_copy(e_recv.at[at], e_recv.at[at], e_sems.at[at]).wait()
        total = e_send[at, core, flat]
        for d in range(31):
            total = total + e_recv[at, d]
        return total

    def send_z(at, d):
        to_space, to_vec = z_peer(d)
        pltpu.make_async_remote_copy(
            src_ref=z_send.at[at], dst_ref=z_recv.at[zee], send_sem=z_sems.at[2],
            recv_sem=z_sems.at[at], device_id=(to_space, to_vec), device_id_type=MESH,
        ).start()

    make_table(0)
    make_table(1)
    for part in range(CHUNKS):
        pltpu.make_async_copy(st_three, st_three, st_sems.at[CHUNKS]).wait()
    send_far()
    phi_near = phi_recv.at[:, 0]
    pltpu.make_async_copy(phi_near, phi_near, own_sem.at[CHUNKS]).wait()
    pltpu.make_async_copy(phi_near, phi_near, phi_recv_sems.at[CHUNKS]).wait()
    total = product(0, half) + product(1, half)
    for n in (2, 3):
        make_table(n)
        total = total + product(n, half)
    scatter(0, total)

    total = None
    for n in range(CHUNKS):
        phi_two = phi_recv.at[n, pl.ds(0, 2)]
        pltpu.make_async_copy(phi_two, phi_two, phi_recv_sems.at[n]).wait()
        term = product(n, 1 - half)
        total = term if total is None else total + term
    scatter(1, total)

    z_send[1] = gathered(1)
    for step in (0, 1, 7, 2, 6, 3, 5, 4):
        send_z(1, (1 - half) * 8 + lax.rem(zlow + step, 8) - zee + 16)

    z_send[0] = gathered(0)
    z_recv[zee] = z_send[0]
    for step in range(1, 8):
        send_z(0, half * 8 + lax.rem(zlow + step, 8) - zee + 16)

    @pl.when(flat != 0)
    def _():
        pltpu.make_async_copy(shift_recv, shift_recv, shift_sems.at[0]).wait()

    @pl.when(flat == 0)
    def _():
        pieces = shift_recv.at[:, pl.ds(0, 15 * LANES)]
        pltpu.make_async_copy(pieces, pieces, shift_sems.at[0]).wait()

    pltpu.make_async_copy(piece, piece, shift_sems.at[3]).wait()

    @pl.when(flat != 15)
    def _():
        pltpu.make_async_copy(piece_low, piece_low, shift_sems.at[5]).wait()

    phi_three = phi_recv.at[:, pl.ds(0, 3)]
    pltpu.make_async_copy(phi_three, phi_three, phi_send_sem.at[0]).wait()
    pltpu.make_async_copy(e_recv, e_recv, e_sems.at[2]).wait()

    z_same = z_recv.at[pl.ds(0, 7)]
    z_other = z_recv.at[pl.ds(0, 8)]
    pltpu.make_async_copy(z_same, z_same, z_sems.at[0]).wait()
    pltpu.make_async_copy(z_other, z_other, z_sems.at[1]).wait()
    whole = z_recv[0]
    for z in range(1, 16):
        whole = whole + z_recv[z]
    mine[...] = whole * (1.0 / math.sqrt(SITES * PLANES))
    place = out.at[lax.div(flat, 8), :, pl.ds(pl.multiple_of(lax.rem(flat, 8) * LANES, LANES), LANES)]
    own_out = pltpu.make_async_copy(mine, place, load_sem.at[0])
    own_out.start()

    for d in FLAT_ORDER:
        if d < 16:
            pltpu.make_async_remote_copy(
                src_ref=mine, dst_ref=place, send_sem=ag_sems.at[0],
                recv_sem=ag_sems.at[1], device_id=flat_peer(d), device_id_type=MESH,
            ).start()

    pltpu.make_async_copy(z_same, z_same, z_sems.at[2]).wait()
    pltpu.make_async_copy(z_other, z_other, z_sems.at[2]).wait()
    own_out.wait()
    ag_others = z_recv.at[pl.ds(0, 15)]
    pltpu.make_async_copy(ag_others, ag_others, ag_sems.at[0]).wait()
    pltpu.make_async_copy(ag_others, ag_others, ag_sems.at[1]).wait()


def shards(vectors, gauge_links, momentum, directions, blocks):
    nblk = vectors.shape[0]
    vec = vectors.transpose(0, 2, 3, 1, 4).reshape(nblk, 48, SITES)
    links = gauge_links.reshape(3, 18, SITES)
    return pl.pallas_call(
        kernel,
        name="elementals",
        out_shape=jax.ShapeDtypeStruct((2, 8, 1024), F32),
        in_specs=[pl.BlockSpec(memory_space=pl.ANY)] * 5,
        out_specs=pl.BlockSpec(memory_space=pl.ANY),
        scratch_shapes=[
            pltpu.SMEM((3,), jnp.int32),
            pltpu.SMEM((2,), jnp.int32),
            pltpu.SMEM((3,), jnp.int32),
            pltpu.VMEM((nblk, 48, SITES), BF16),
            pltpu.VMEM((3, 18, SITES), BF16),
            pltpu.VMEM((CHUNKS, 4, 96, LANES), BF16),
            pltpu.VMEM((CHUNKS, 4, 96, LANES), BF16),
            pltpu.VMEM((4, 96, LANES), F32),
            pltpu.VMEM((48, SITES), F32),
            pltpu.VMEM((48, SITES), BF16),
            pltpu.VMEM((48, SITES), BF16),
            pltpu.VMEM((48, LANES), BF16),
            pltpu.VMEM((48, LANES), BF16),
            pltpu.VMEM((8, SITES), F32),
            pltpu.VMEM((8, SITES), F32),
            pltpu.VMEM((CHUNKS, 4, 48, LANES), BF16),
            pltpu.VMEM((CHUNKS, 4, 48, LANES), BF16),
            pltpu.VMEM((CHUNKS, 1024, 6 * LANES), BF16),
            pltpu.VMEM((2, 2, 16, 8, LANES), F32),
            pltpu.VMEM((2, 31, 8, LANES), F32),
            pltpu.VMEM((2, 8, LANES), F32),
            pltpu.VMEM((16, 8, LANES), F32),
            pltpu.VMEM((8, LANES), F32),
            pltpu.SemaphoreType.DMA((4 + nblk,)),
            pltpu.SemaphoreType.DMA((CHUNKS + 1,)),
            pltpu.SemaphoreType.DMA((6,)),
            pltpu.SemaphoreType.DMA((CHUNKS + 1,)),
            pltpu.SemaphoreType.DMA((1,)),
            pltpu.SemaphoreType.DMA((CHUNKS + 1,)),
            pltpu.SemaphoreType.DMA((3,)),
            pltpu.SemaphoreType.DMA((3,)),
            pltpu.SemaphoreType.DMA((2,)),
            pltpu.SemaphoreType.REGULAR((3,)),
        ],
        compiler_params=pltpu.CompilerParams(
            collective_id=1, has_side_effects=True, vmem_limit_bytes=63 * 2**20
        ),
    )(momentum, directions, blocks, vec, links)


def solution(mesh):
    in_specs = (P(None, "vec", None, "space", None), P(None, None, "space", None), P(), P(), P())
    out_specs = P(None, "vec", None)
    return jax.shard_map(shards, mesh=mesh, in_specs=in_specs, out_specs=out_specs, check_vma=False)
```
